512 devices in a mesh: wide: 64 (over x, z_hi, y, core), narrow: 8 (over z_lo).
Axes of the slice: x: 4, y: 4, z: 16 (z_hi: 2, z_lo: 8; z = z_hi * 8 + z_lo), core: 2. Of those that a mesh axis runs over, the one named last changes fastest.
Arguments:
- pair_rep: bfloat16 [512, 512, 128], P('wide', 'narrow'), may hold values from -6 to 6
- pair_gain: float32 [128], replicated, may hold values from 0.1 to 1.9
- pair_bias: float32 [128], replicated, may hold values from -3 to 3
- left_weight: bfloat16 [128, 256], replicated, may hold values from -0.5 to 0.5
- right_weight: bfloat16 [128, 256], replicated, may hold values from -0.5 to 0.5
- gate_weight: bfloat16 [128, 128], replicated, may hold values from -0.5 to 0.5
- out_weight: bfloat16 [128, 128], replicated, may hold values from -0.5 to 0.5
- out_gain: float32 [128], replicated, may hold values from 0.1 to 1.9
- out_bias: float32 [128], replicated, may hold values from -3 to 3
Outputs:
- update_t: bfloat16 [512, 128, 512], P('wide', 'narrow')
The draws below stay inside these ranges and needn't reach their ends.
All inputs are finite; a program needn't handle non-finite values.
Results may differ from the reference program's by a relative error of at most 0.0053.
Values may be sent and summed in bfloat16 or wider, within the bound.
No kernel may reach another device: no remote copies, remote signals or barrier semaphores. Data moves between devices by JAX's collectives and lax.ppermute only.
A program may use at most 64 MiB of HBM per device.

```python
import jax
import jax.numpy as jnp
from jax import lax

C = 128
H = 128
N = 512


def levels(own_key, extent, split, low, top_value):
    level, own = 1.0, jax.random.fold_in(own_key, 6)
    for dim, blocks in split:
        draws = jnp.exp(jax.random.uniform(jax.random.fold_in(own, dim), (blocks,), jnp.float32, low / len(split), top_value / len(split)))
        level = level * jnp.repeat(draws, extent[dim] // blocks).reshape([-1 if axis == dim else 1 for axis in range(len(extent))])
    return level


def gaussian(own_key, shape, scale, bound, split=(), dtype=jnp.bfloat16):
    level = levels(own_key, shape, split, -0.22, 0.18) if split else 1.0
    values = jax.random.normal(own_key, shape, jnp.float32) * scale * level
    return jnp.minimum(jnp.maximum(values, -bound), bound).astype(dtype)


def setup_inputs(seed: int = 0) -> dict:
    keys = jax.random.split(jax.random.key(seed), 10)
    pair_rep = gaussian(keys[0], (N, N, C), 1.0, 6.0, ((0, 64), (1, 8)))
    pair_gain = jnp.clip(1.0 + 0.18 * jax.random.normal(keys[1], (C,), jnp.float32), 0.1, 1.9)
    pair_bias = gaussian(keys[2], (C,), 0.5, 3.0, (), jnp.float32)
    left_weight = gaussian(keys[3], (C, 2 * H), C ** -0.5, 0.5)
    right_weight = gaussian(keys[4], (C, 2 * H), C ** -0.5, 0.5)
    gate_weight = gaussian(keys[5], (C, C), C ** -0.5, 0.5)
    out_weight = gaussian(keys[6], (H, C), H ** -0.5, 0.5)
    out_gain = jnp.clip(1.0 + 0.18 * jax.random.normal(keys[7], (H,), jnp.float32), 0.1, 1.9)
    out_bias = gaussian(keys[8], (H,), 0.5, 3.0, (), jnp.float32)
    return {"pair_rep": pair_rep, "pair_gain": pair_gain, "pair_bias": pair_bias, "left_weight": left_weight, "right_weight": right_weight, "gate_weight": gate_weight, "out_weight": out_weight, "out_gain": out_gain, "out_bias": out_bias}


def layer_norm(values, gain, bias):
    center = lax.optimization_barrier(jnp.mean(values, axis=-1, keepdims=True))
    spread = lax.optimization_barrier(jnp.mean((values - center) ** 2, axis=-1, keepdims=True))
    return (values - center) * jax.lax.rsqrt(spread + 1e-05) * gain + bias

def edge_values(pair_normed, weight):
    flat = jnp.dot(pair_normed.reshape(N * N, C), weight, preferred_element_type=jnp.float32)
    flat = flat.reshape(N, N, 2 * H)
    return (jax.nn.sigmoid(flat[:, :, H:]) * flat[:, :, :H]).astype(jnp.bfloat16)

def reference(pair_rep, pair_gain, pair_bias, left_weight, right_weight, gate_weight, out_weight, out_gain, out_bias):
    pair_normed = layer_norm(pair_rep.astype(jnp.float32), pair_gain, pair_bias).astype(jnp.bfloat16)
    left_edge = jnp.transpose(edge_values(pair_normed, left_weight), (2, 0, 1)).astype(jnp.float32)
    right_edge = jnp.transpose(edge_values(pair_normed, right_weight), (2, 0, 1)).astype(jnp.float32)
    triangle = jnp.einsum('hik,hjk->hij', left_edge, right_edge)
    center = lax.optimization_barrier(jnp.sum(triangle, axis=0)) / H
    spread = lax.optimization_barrier(jnp.sum(triangle * triangle, axis=0)) / H - center * center
    tri_normed = (triangle - center) * jax.lax.rsqrt(spread + 1e-05)
    tri_normed = (tri_normed * out_gain[:, None, None] + out_bias[:, None, None]).astype(jnp.bfloat16)
    projected = jnp.einsum('hij,hc->ijc', tri_normed.astype(jnp.float32), out_weight.astype(jnp.float32))
    gate_logit = jnp.dot(pair_normed.reshape(N * N, C), gate_weight, preferred_element_type=jnp.float32)
    out_gate = jax.nn.sigmoid(gate_logit.reshape(N, N, C))
    update = out_gate * projected
    return jnp.transpose(update, (1, 2, 0)).astype(jnp.bfloat16)
```

```python
import jax
import jax.numpy as jnp
import numpy as np
from jax import lax
from jax.experimental import pallas as pl
from jax.experimental.pallas import tpu as pltpu
from jax.sharding import Mesh, PartitionSpec as P

F32 = jnp.float32
BF16 = jnp.bfloat16
ROWS = 8
SPLIT = ("n", "zh", "y")


def params():
    return pltpu.CompilerParams(vmem_limit_bytes=48 * 1024 * 1024)


def lane_mask(shape):
    return lax.broadcasted_iota(jnp.int32, shape, len(shape) - 1) < 64


def swap_halves(values):
    return pltpu.roll(values, 64, len(values.shape) - 1)


def edges_kernel(pair, gain, bias, left_weight, right_weight, edges, normed, scratch, gate_rows):
    values = pair[...].astype(F32).reshape(512, 128)
    center = jnp.mean(values, axis=-1, keepdims=True)
    moved = values - center
    spread = jnp.mean(moved * moved, axis=-1, keepdims=True)
    scaled = moved * lax.rsqrt(spread + 1e-05) * gain[...] + bias[...]
    rounded = scaled.astype(BF16)
    for row in range(ROWS):
        gate_rows[pl.ds(row, 64, stride=ROWS), :] = scaled[row * 64 : row * 64 + 64]
    normed[...] = gate_rows[...].astype(BF16)
    for side, weight in enumerate((left_weight, right_weight)):
        both = lax.dot_general(
            weight[...], rounded, (((0,), (1,)), ((), ())), preferred_element_type=F32
        )
        edge = jax.nn.sigmoid(both[128:]) * both[:128]
        for pair_of_rows in range(4):
            lanes = slice(pair_of_rows * 128, pair_of_rows * 128 + 128)
            first, second = edge[:64, lanes], edge[64:, lanes]
            low = lane_mask(first.shape)
            even = jnp.where(low, first, swap_halves(second))
            odd = jnp.where(low, swap_halves(first), second)
            start = side * 8 + pair_of_rows * 2
            scratch[pl.ds(start, 64, stride=16), :] = even
            scratch[pl.ds(start + 1, 64, stride=16), :] = odd
    edges[...] = scratch[...].astype(BF16)


def make_edges(pair, gain, bias, left_weight, right_weight):
    return pl.pallas_call(
        edges_kernel,
        out_shape=(
            jax.ShapeDtypeStruct((1024, 128), BF16),
            jax.ShapeDtypeStruct((512, 128), BF16),
        ),
        scratch_shapes=[pltpu.VMEM((1024, 128), F32), pltpu.VMEM((512, 128), F32)],
        compiler_params=params(),
        name="edges",
    )(pair, gain.reshape(1, 128), bias.reshape(1, 128), left_weight, right_weight)


def triangle_kernel(core, own, other, edges, out):
    first_core = core[0] == 0
    total = jnp.zeros((128, 512), F32)
    for part in range(8):
        mine = own[:, part].astype(F32).reshape(32, 8, 128)
        theirs = other[:, part].astype(F32).reshape(32, 8, 128)
        rows = jnp.concatenate(
            [jnp.where(first_core, mine, theirs), jnp.where(first_core, theirs, mine)], axis=1
        )
        left = rows.reshape(512, 128).astype(BF16)
        right = edges[part].astype(F32)[:, 8:].reshape(64, 128)
        low = lane_mask(right.shape)
        right = jnp.concatenate(
            [jnp.where(low, right, 0.0), jnp.where(low, 0.0, right)], axis=0
        ).astype(BF16)
        total += lax.dot_general(
            right, left, (((1,), (1,)), ((), ())), preferred_element_type=F32
        )
    shape = (64, 128)
    low = lane_mask(shape)
    upper = lax.broadcasted_iota(jnp.int32, shape, 0) % 8 < 4
    for block in range(4):
        columns = total[:, block * 128 : block * 128 + 128]
        turned = []
        for hidden in range(2):
            held = columns[hidden * 64 : hidden * 64 + 64]
            up, down = pltpu.roll(held, 60, 0), pltpu.roll(held, 4, 0)
            crossed = swap_halves(jnp.where(upper, up, down))
            turned.append(jnp.where(upper == low, held, crossed))
        even = jnp.where(upper, turned[0], pltpu.roll(turned[1], 4, 0))
        odd = jnp.where(upper, pltpu.roll(turned[0], 60, 0), turned[1])
        out[block * 2] = even.astype(BF16)
        out[block * 2 + 1] = odd.astype(BF16)


def make_triangle(core, own, other, edges):
    return pl.pallas_call(
        triangle_kernel,
        out_shape=jax.ShapeDtypeStruct((8, 64, 128), BF16),
        in_specs=[pl.BlockSpec(memory_space=pltpu.SMEM)]
        + [pl.BlockSpec(memory_space=pltpu.VMEM)] * 3,
        compiler_params=params(),
        name="triangle",
    )(core, own, other, edges)


def update_kernel(triangle, normed, gate_weight, out_weight, gain, bias, out, scratch):
    values = triangle[...].astype(F32)
    sums = jnp.sum(values, axis=0)
    squares = jnp.sum(values * values, axis=0)
    center = (sums + pltpu.roll(sums, 4, 0)) / 128
    spread = (squares + pltpu.roll(squares, 4, 0)) / 128 - center * center
    scale = lax.rsqrt(spread + 1e-05)
    scratch[...] = ((values - center) * scale).reshape(512, 128)
    tall_gain = jnp.transpose(jnp.broadcast_to(gain[...], (128, 128)))
    tall_bias = jnp.transpose(jnp.broadcast_to(bias[...], (128, 128)))
    for part in range(4):
        held = jnp.concatenate(
            [
                scratch[pl.ds(part, 64, stride=8), :],
                scratch[pl.ds(4 + part, 64, stride=8), :],
            ],
            axis=0,
        )
        held = (held * tall_gain + tall_bias).astype(BF16)
        projected = lax.dot_general(
            out_weight[...], held, (((0,), (0,)), ((), ())), preferred_element_type=F32
        )
        rows = jnp.concatenate(
            [
                normed[:, part].astype(F32).reshape(64, 128),
                normed[:, 4 + part].astype(F32).reshape(64, 128),
            ],
            axis=0,
        ).astype(BF16)
        logits = lax.dot_general(
            gate_weight[...], rows, (((0,), (1,)), ((), ())), preferred_element_type=F32
        )
        update = (jax.nn.sigmoid(logits) * projected).astype(BF16)
        out[:, part] = update.reshape(8, 16, 128)


def make_update(triangle, normed, gate_weight, out_weight, gain, bias):
    return pl.pallas_call(
        update_kernel,
        out_shape=jax.ShapeDtypeStruct((8, 4, 16, 128), BF16),
        scratch_shapes=[pltpu.VMEM((512, 128), F32)],
        compiler_params=params(),
        name="update",
    )(triangle, normed, gate_weight, out_weight, gain.reshape(1, 128), bias.reshape(1, 128))


def order_kernel(update, out):
    for block in range(4):
        first = update[block * 2].astype(F32).reshape(64, 128)
        second = update[block * 2 + 1].astype(F32).reshape(64, 128)
        low = lane_mask(first.shape)
        upper = jnp.where(low, first, swap_halves(second)).astype(BF16)
        lower = jnp.where(low, swap_halves(first), second).astype(BF16)
        lanes = slice(block * 128, block * 128 + 128)
        out[:4, :, lanes] = upper.reshape(4, 16, 128)
        out[4:, :, lanes] = lower.reshape(4, 16, 128)


def make_order(update):
    return pl.pallas_call(
        order_kernel,
        out_shape=jax.ShapeDtypeStruct((8, 16, 512), BF16),
        compiler_params=params(),
        name="order",
    )(update)


def exchange(values, axes):
    return lax.all_to_all(values, axes, 0, 0, tiled=True)


def shards(
    pair_rep,
    pair_gain,
    pair_bias,
    left_weight,
    right_weight,
    gate_weight,
    out_weight,
    out_gain,
    out_bias,
):
    edges, normed = make_edges(pair_rep, pair_gain, pair_bias, left_weight, right_weight)
    swapped = [((a * 8 + e) * 8 + n, (n * 8 + e) * 8 + a) for a in range(8) for e in range(8) for n in range(8)]
    normed = exchange(normed.reshape(8, 8, 8, 128), ("y", "co"))
    normed = lax.ppermute(normed, ("x", "zh", "y", "co", "n"), swapped)
    edges = exchange(edges.reshape(64, 16, 128), SPLIT).reshape(8, 8, 16, 128)
    left = edges[:, :, :8]
    own = exchange(jnp.broadcast_to(left[None], (4,) + left.shape), "x")
    other = lax.ppermute(own, "co", [(0, 1), (1, 0)])
    core = lax.axis_index("co").astype(jnp.int32).reshape(1)
    triangle = make_triangle(core, own, other, edges)
    triangle = exchange(triangle.reshape(64, 8, 128), SPLIT)
    update = make_update(triangle, normed, gate_weight, out_weight, out_gain, out_bias)
    return make_order(exchange(update, "n"))


def solution(mesh):
    fine = Mesh(mesh.devices.reshape(4, 2, 4, 2, 8), ("x", "zh", "y", "co", "n"))
    rows = ("x", "zh", "y", "co")
    in_specs = (P(rows, "n", None), P(), P(), P(), P(), P(), P(), P(), P())
    out_specs = P(rows, "n", None)
    return jax.shard_map(shards, mesh=fine, in_specs=in_specs, out_specs=out_specs, check_vma=False)
```

```python
import jax
import jax.numpy as jnp
from jax import lax
from jax.experimental import pallas as pl
from jax.experimental.pallas import tpu as pltpu
from jax.sharding import Mesh, PartitionSpec as P

F32 = jnp.float32
BF16 = jnp.bfloat16
ROWS = 8
AXES = ("x", "zh", "y", "co", "n")
SPLIT = ("n", "x", "zh")


def params(mib=16):
    return pltpu.CompilerParams(vmem_limit_bytes=mib * 1024 * 1024)


def lane_mask(shape):
    return lax.broadcasted_iota(jnp.int32, shape, len(shape) - 1) < 64


def swap_halves(values):
    return pltpu.roll(values, 64, len(values.shape) - 1)


def cross_halves(first, second):
    low = lane_mask(first.shape)
    return (
        jnp.where(low, first, swap_halves(second)),
        jnp.where(low, swap_halves(first), second),
    )


def layer_norm(values, gain, bias):
    center = jnp.mean(values, axis=-1, keepdims=True)
    moved = values - center
    spread = jnp.mean(moved * moved, axis=-1, keepdims=True)
    return moved * lax.rsqrt(spread + 1e-05) * gain + bias


def edges_kernel(
    pair_hbm, gain_hbm, bias_hbm, left_hbm, right_hbm, last_gain_hbm, last_bias_hbm,
    edges, normed, tall, pair, gain, bias, left_weight, right_weight, last_gain, last_bias, scratch, sems,
):
    moves = [
        pltpu.make_async_copy(source, target, sems.at[slot])
        for slot, (source, target) in enumerate(
            (
                (pair_hbm, pair),
                (gain_hbm, gain),
                (bias_hbm, bias),
                (left_hbm, left_weight),
                (right_hbm, right_weight),
                (last_gain_hbm, last_gain),
                (last_bias_hbm, last_bias),
            )
        )
    ]
    for move in moves:
        move.start()
    for move in moves:
        move.wait()
    values = pair[...].astype(F32).reshape(512, 128)
    rounded = layer_norm(values, gain[...], bias[...]).astype(BF16)
    normed[...] = rounded
    for side, weight in enumerate((left_weight, right_weight)):
        both = lax.dot_general(
            weight[...], rounded, (((0,), (1,)), ((), ())), preferred_element_type=F32
        )
        edge = jax.nn.sigmoid(both[128:]) * both[:128]
        for block in range(4):
            lanes = slice(block * 128, block * 128 + 128)
            even, odd = cross_halves(edge[:64, lanes], edge[64:, lanes])
            start = side * 8 + block * 2
            scratch[pl.ds(start, 64, stride=16), :] = even
            scratch[pl.ds(start + 1, 64, stride=16), :] = odd
    edges[...] = scratch[...].astype(BF16)
    tall[0] = jnp.transpose(jnp.broadcast_to(last_gain[...], (128, 128)))
    tall[1] = jnp.transpose(jnp.broadcast_to(last_bias[...], (128, 128)))


def make_edges(pair, gain, bias, left_weight, right_weight, last_gain, last_bias):
    row = pltpu.VMEM((1, 128), F32)
    return pl.pallas_call(
        edges_kernel,
        out_shape=(
            jax.ShapeDtypeStruct((1024, 128), BF16),
            jax.ShapeDtypeStruct((512, 128), BF16),
            jax.ShapeDtypeStruct((2, 128, 128), F32),
        ),
        in_specs=[pl.BlockSpec(memory_space=pltpu.HBM)] * 7,
        scratch_shapes=[
            pltpu.VMEM((8, 64, 128), BF16),
            row,
            row,
            pltpu.VMEM((128, 256), BF16),
            pltpu.VMEM((128, 256), BF16),
            row,
            row,
            pltpu.VMEM((1024, 128), F32),
            pltpu.SemaphoreType.DMA((7,)),
        ],
        compiler_params=params(63),
        name="edges",
    )(
        pair,
        gain.reshape(1, 128),
        bias.reshape(1, 128),
        left_weight,
        right_weight,
        last_gain.reshape(1, 128),
        last_bias.reshape(1, 128),
    )


def pack_kernel(edges, pair, payload):
    left = edges[:, :8].reshape(512, 128)
    for target in range(4):
        payload[target, :512] = left
        payload[target, 512:] = pair[:, target * 16 : target * 16 + 16].reshape(128, 128)


def make_pack(edges, pair):
    return pl.pallas_call(
        pack_kernel,
        out_shape=jax.ShapeDtypeStruct((4, 640, 128), BF16),
        compiler_params=params(),
        name="pack",
    )(edges, pair)


def triangle_kernel(
    core, own, other, edges, gate_weight, out, gates, normed
):
    first_core = core[0] == 0
    total = jnp.zeros((128, 512), F32)
    for part in range(8):
        rows = slice(part * 64, part * 64 + 64)
        mine = own[:, rows].astype(F32).reshape(4, 8, 8, 128)
        theirs = other[:, rows].astype(F32).reshape(4, 8, 8, 128)
        first = jnp.where(first_core, mine, theirs)
        second = jnp.where(first_core, theirs, mine)
        left = jnp.concatenate(
            [held[y, a] for a in range(8) for y in range(4) for held in (first, second)], axis=0
        ).astype(BF16)
        right = edges[part].astype(F32)[:, 8:].reshape(64, 128)
        low = lane_mask(right.shape)
        right = jnp.concatenate(
            [jnp.where(low, right, 0.0), jnp.where(low, 0.0, right)], axis=0
        ).astype(BF16)
        total += lax.dot_general(
            right, left, (((1,), (1,)), ((), ())), preferred_element_type=F32
        )
    shape = (64, 128)
    low = lane_mask(shape)
    upper = lax.broadcasted_iota(jnp.int32, shape, 0) % 8 < 4
    for block in range(4):
        columns = total[:, block * 128 : block * 128 + 128]
        turned = []
        for hidden in range(2):
            held = columns[hidden * 64 : hidden * 64 + 64]
            up, down = pltpu.roll(held, 60, 0), pltpu.roll(held, 4, 0)
            crossed = swap_halves(jnp.where(upper, up, down))
            turned.append(jnp.where(upper == low, held, crossed))
        even = jnp.where(upper, turned[0], pltpu.roll(turned[1], 4, 0))
        odd = jnp.where(upper, pltpu.roll(turned[0], 60, 0), turned[1])
        out[block * 2] = even.astype(BF16)
        out[block * 2 + 1] = odd.astype(BF16)
    mine = own[:, 512:].astype(F32).reshape(32, 16, 128)
    theirs = other[:, 512:].astype(F32).reshape(32, 16, 128)
    mine = jnp.where(first_core, mine[:, :8], mine[:, 8:]).reshape(4, 64, 128)
    theirs = jnp.where(first_core, theirs[:, :8], theirs[:, 8:]).reshape(4, 64, 128)
    first = jnp.where(first_core, mine, theirs)
    second = jnp.where(first_core, theirs, mine)
    rows = jnp.concatenate([first, second], axis=1).reshape(512, 128)
    normed[...] = rows
    for part in range(4):
        rows = jnp.concatenate(
            [normed[pl.ds(part, 64, stride=8), :], normed[pl.ds(4 + part, 64, stride=8), :]],
            axis=0,
        ).astype(BF16)
        logits = lax.dot_general(
            gate_weight[...], rows, (((0,), (1,)), ((), ())), preferred_element_type=F32
        )
        gates[part] = jax.nn.sigmoid(logits)


def make_triangle(core, own, other, edges, gate_weight):
    return pl.pallas_call(
        triangle_kernel,
        out_shape=(
            jax.ShapeDtypeStruct((8, 64, 128), BF16),
            jax.ShapeDtypeStruct((4, 128, 128), F32),
        ),
        in_specs=[pl.BlockSpec(memory_space=pltpu.SMEM)]
        + [pl.BlockSpec(memory_space=pltpu.VMEM)] * 4,
        scratch_shapes=[pltpu.VMEM((512, 128), F32)],
        compiler_params=params(),
        name="triangle",
    )(core, own, other, edges, gate_weight)


def update_kernel(triangle, gates, out_weight, tall, out, scratch):
    values = triangle[...].astype(F32)
    sums = jnp.sum(values, axis=0)
    squares = jnp.sum(values * values, axis=0)
    center = (sums + pltpu.roll(sums, 4, 0)) / 128
    spread = (squares + pltpu.roll(squares, 4, 0)) / 128 - center * center
    scale = lax.rsqrt(spread + 1e-05)
    scratch[...] = ((values - center) * scale).reshape(512, 128)
    for part in range(4):
        held = jnp.concatenate(
            [
                scratch[pl.ds(part, 64, stride=8), :],
                scratch[pl.ds(4 + part, 64, stride=8), :],
            ],
            axis=0,
        )
        held = (held * tall[0] + tall[1]).astype(BF16)
        projected = lax.dot_general(
            out_weight[...], held, (((0,), (0,)), ((), ())), preferred_element_type=F32
        )
        out[:, part] = (gates[part] * projected).astype(BF16).reshape(8, 16, 128)


def make_update(triangle, gates, out_weight, tall):
    return pl.pallas_call(
        update_kernel,
        out_shape=jax.ShapeDtypeStruct((8, 4, 16, 128), BF16),
        scratch_shapes=[pltpu.VMEM((512, 128), F32)],
        compiler_params=params(),
        name="update",
    )(triangle, gates, out_weight, tall)


def order_kernel(update, out):
    for block in range(4):
        first = update[block * 2].astype(F32).reshape(64, 128)
        second = update[block * 2 + 1].astype(F32).reshape(64, 128)
        upper, lower = cross_halves(first, second)
        lanes = slice(block * 128, block * 128 + 128)
        out[:4, :, lanes] = upper.astype(BF16).reshape(4, 16, 128)
        out[4:, :, lanes] = lower.astype(BF16).reshape(4, 16, 128)


def make_order(update):
    return pl.pallas_call(
        order_kernel,
        out_shape=jax.ShapeDtypeStruct((8, 16, 512), BF16),
        compiler_params=params(),
        name="order",
    )(update)


def exchange(values, axes):
    return lax.all_to_all(values, axes, 0, 0, tiled=True)


def shards(
    pair_rep,
    pair_gain,
    pair_bias,
    left_weight,
    right_weight,
    gate_weight,
    out_weight,
    out_gain,
    out_bias,
):
    swapped = [
        ((a * 8 + e) * 8 + n, (n * 8 + e) * 8 + a)
        for a in range(8)
        for e in range(8)
        for n in range(8)
    ]
    core = lax.axis_index("co").astype(jnp.int32).reshape(1)
    edges, normed, tall = make_edges(
        pair_rep, pair_gain, pair_bias, left_weight, right_weight, out_gain, out_bias
    )
    moved = lax.ppermute(normed.reshape(8, 64, 128), AXES, swapped)
    edges = lax.cond(
        lax.axis_index("x") < 4,
        lambda held: exchange(held, SPLIT),
        lambda held: held,
        edges.reshape(64, 16, 128),
    )
    own = exchange(make_pack(edges, moved), "y")
    other = lax.ppermute(own, "co", [(0, 1), (1, 0)])
    triangle, gates = make_triangle(
        core, own, other, edges.reshape(8, 8, 16, 128), gate_weight
    )
    triangle = exchange(triangle.reshape(64, 8, 128), SPLIT)
    update = make_update(triangle, gates, out_weight, tall)
    return make_order(exchange(update, "n"))


def solution(mesh):
    fine = Mesh(mesh.devices.reshape(4, 2, 4, 2, 8), AXES)
    rows = ("x", "zh", "y", "co")
    in_specs = (P(rows, "n", None), P(), P(), P(), P(), P(), P(), P(), P())
    out_specs = P(rows, "n", None)
    return jax.shard_map(shards, mesh=fine, in_specs=in_specs, out_specs=out_specs, check_vma=False)
```

```python
import jax
import jax.numpy as jnp
from jax import lax
from jax.experimental import pallas as pl
from jax.experimental.pallas import tpu as pltpu
from jax.sharding import Mesh, PartitionSpec as P

F32 = jnp.float32
BF16 = jnp.bfloat16
ROWS = 8
AXES = ("x", "zh", "y", "co", "n")
SPLIT = ("n", "x", "zh")


PLACES = (
    (3, 4, 1, 5, 0, 7, 2, 6),
    (4, 3, 5, 0, 7, 1, 6, 2),
    (1, 5, 0, 4, 3, 6, 2, 7),
    (0, 2, 1, 5, 6, 4, 7, 3),
    (4, 0, 3, 1, 2, 6, 5, 7),
    (0, 5, 1, 4, 3, 7, 2, 6),
    (5, 1, 6, 0, 7, 2, 4, 3),
    (1, 5, 0, 7, 2, 6, 3, 4),
)


def params(mib=16):
    return pltpu.CompilerParams(vmem_limit_bytes=mib * 1024 * 1024)


def lane_mask(shape):
    return lax.broadcasted_iota(jnp.int32, shape, len(shape) - 1) < 64


def swap_halves(values):
    return pltpu.roll(values, 64, len(values.shape) - 1)


def cross_halves(first, second):
    low = lane_mask(first.shape)
    return (
        jnp.where(low, first, swap_halves(second)),
        jnp.where(low, swap_halves(first), second),
    )


def layer_norm(values, gain, bias):
    center = jnp.mean(values, axis=-1, keepdims=True)
    moved = values - center
    spread = jnp.mean(moved * moved, axis=-1, keepdims=True)
    return moved * lax.rsqrt(spread + 1e-05) * gain + bias


def edges_kernel(
    pair_hbm, gain_hbm, bias_hbm, left_hbm, right_hbm, last_gain_hbm, last_bias_hbm,
    edges, normed, tall, pair, gain, bias, left_weight, right_weight, last_gain, last_bias, scratch, sems,
):
    moves = [
        pltpu.make_async_copy(source, target, sems.at[slot])
        for slot, (source, target) in enumerate(
            (
                (pair_hbm, pair),
                (gain_hbm, gain),
                (bias_hbm, bias),
                (left_hbm, left_weight),
                (right_hbm, right_weight),
                (last_gain_hbm, last_gain),
                (last_bias_hbm, last_bias),
            )
        )
    ]
    for move in moves:
        move.start()
    for move in moves:
        move.wait()
    values = pair[...].astype(F32).reshape(512, 128)
    rounded = layer_norm(values, gain[...], bias[...]).astype(BF16)
    normed[...] = rounded
    for side, weight in enumerate((left_weight, right_weight)):
        both = lax.dot_general(
            weight[...], rounded, (((0,), (1,)), ((), ())), preferred_element_type=F32
        )
        edge = jax.nn.sigmoid(both[128:]) * both[:128]
        for block in range(4):
            lanes = slice(block * 128, block * 128 + 128)
            even, odd = cross_halves(edge[:64, lanes], edge[64:, lanes])
            start = side * 8 + block * 2
            scratch[pl.ds(start, 64, stride=16), :] = even
            scratch[pl.ds(start + 1, 64, stride=16), :] = odd
    edges[...] = scratch[...].astype(BF16)
    tall[0] = jnp.transpose(jnp.broadcast_to(last_gain[...], (128, 128)))
    tall[1] = jnp.transpose(jnp.broadcast_to(last_bias[...], (128, 128)))


def make_edges(pair, gain, bias, left_weight, right_weight, last_gain, last_bias):
    row = pltpu.VMEM((1, 128), F32)
    return pl.pallas_call(
        edges_kernel,
        out_shape=(
            jax.ShapeDtypeStruct((1024, 128), BF16),
            jax.ShapeDtypeStruct((512, 128), BF16),
            jax.ShapeDtypeStruct((2, 128, 128), F32),
        ),
        in_specs=[pl.BlockSpec(memory_space=pltpu.HBM)] * 7,
        scratch_shapes=[
            pltpu.VMEM((8, 64, 128), BF16),
            row,
            row,
            pltpu.VMEM((128, 256), BF16),
            pltpu.VMEM((128, 256), BF16),
            row,
            row,
            pltpu.VMEM((1024, 128), F32),
            pltpu.SemaphoreType.DMA((7,)),
        ],
        compiler_params=params(63),
        name="edges",
    )(
        pair,
        gain.reshape(1, 128),
        bias.reshape(1, 128),
        left_weight,
        right_weight,
        last_gain.reshape(1, 128),
        last_bias.reshape(1, 128),
    )


def pack_kernel(edges, pair, payload):
    left = edges[:, :8].reshape(512, 128)
    for target in range(4):
        payload[target, :512] = left
        payload[target, 512:] = pair[:, target * 16 : target * 16 + 16].reshape(128, 128)


def make_pack(edges, pair):
    return pl.pallas_call(
        pack_kernel,
        out_shape=jax.ShapeDtypeStruct((4, 640, 128), BF16),
        compiler_params=params(),
        name="pack",
    )(edges, pair)


def triangle_kernel(
    place, own, other, edges, gate_weight, out, gates, normed
):
    first_core = place[0] % 2 == 0
    total = jnp.zeros((128, 512), F32)
    for part in range(8):
        rows = slice(part * 64, part * 64 + 64)
        mine = own[:, rows].astype(F32).reshape(4, 8, 8, 128)
        theirs = other[:, rows].astype(F32).reshape(4, 8, 8, 128)
        first = jnp.where(first_core, mine, theirs)
        second = jnp.where(first_core, theirs, mine)
        left = jnp.concatenate(
            [held[y, a] for a in range(8) for y in range(4) for held in (first, second)], axis=0
        ).astype(BF16)
        right = edges[part].astype(F32)[:, 8:].reshape(64, 128)
        low = lane_mask(right.shape)
        right = jnp.concatenate(
            [jnp.where(low, right, 0.0), jnp.where(low, 0.0, right)], axis=0
        ).astype(BF16)
        total += lax.dot_general(
            right, left, (((1,), (1,)), ((), ())), preferred_element_type=F32
        )
    shape = (64, 128)
    low = lane_mask(shape)
    upper = lax.broadcasted_iota(jnp.int32, shape, 0) % 8 < 4
    for block in range(4):
        columns = total[:, block * 128 : block * 128 + 128]
        turned = []
        for hidden in range(2):
            held = columns[hidden * 64 : hidden * 64 + 64]
            up, down = pltpu.roll(held, 60, 0), pltpu.roll(held, 4, 0)
            crossed = swap_halves(jnp.where(upper, up, down))
            turned.append(jnp.where(upper == low, held, crossed))
        even = jnp.where(upper, turned[0], pltpu.roll(turned[1], 4, 0))
        odd = jnp.where(upper, pltpu.roll(turned[0], 60, 0), turned[1])
        for side, rows in enumerate((even, odd)):
            rows = rows.astype(BF16).reshape(8, 8, 128)
            for target in range(8):
                out[PLACES[target][block * 2 + side], target] = rows[target]
    mine = own[:, 512:].astype(F32).reshape(32, 16, 128)
    theirs = other[:, 512:].astype(F32).reshape(32, 16, 128)
    mine = jnp.where(first_core, mine[:, :8], mine[:, 8:]).reshape(4, 64, 128)
    theirs = jnp.where(first_core, theirs[:, :8], theirs[:, 8:]).reshape(4, 64, 128)
    first = jnp.where(first_core, mine, theirs)
    second = jnp.where(first_core, theirs, mine)
    rows = jnp.concatenate([first, second], axis=1).reshape(512, 128)
    normed[...] = rows
    for part in range(4):
        rows = jnp.concatenate(
            [normed[pl.ds(part, 64, stride=8), :], normed[pl.ds(4 + part, 64, stride=8), :]],
            axis=0,
        ).astype(BF16)
        logits = lax.dot_general(
            gate_weight[...], rows, (((0,), (1,)), ((), ())), preferred_element_type=F32
        )
        gates[part] = jax.nn.sigmoid(logits)


def make_triangle(place, own, other, edges, gate_weight):
    return pl.pallas_call(
        triangle_kernel,
        out_shape=(
            jax.ShapeDtypeStruct((8, 8, 8, 128), BF16),
            jax.ShapeDtypeStruct((4, 128, 128), F32),
        ),
        in_specs=[pl.BlockSpec(memory_space=pltpu.SMEM)]
        + [pl.BlockSpec(memory_space=pltpu.VMEM)] * 4,
        scratch_shapes=[pltpu.VMEM((512, 128), F32)],
        compiler_params=params(),
        name="triangle",
    )(place, own, other, edges, gate_weight)


def update_kernel(triangle, gates, out_weight, tall, out, scratch):
    values = triangle[...].astype(F32)
    sums = jnp.sum(values, axis=0)
    squares = jnp.sum(values * values, axis=0)
    center = (sums + pltpu.roll(sums, 4, 0)) / 128
    spread = (squares + pltpu.roll(squares, 4, 0)) / 128 - center * center
    scale = lax.rsqrt(spread + 1e-05)
    scratch[...] = ((values - center) * scale).reshape(512, 128)
    for part in range(4):
        held = jnp.concatenate(
            [
                scratch[pl.ds(part, 64, stride=8), :],
                scratch[pl.ds(4 + part, 64, stride=8), :],
            ],
            axis=0,
        )
        held = (held * tall[0] + tall[1]).astype(BF16)
        projected = lax.dot_general(
            out_weight[...], held, (((0,), (0,)), ((), ())), preferred_element_type=F32
        )
        out[:, part] = (gates[part] * projected).astype(BF16).reshape(8, 16, 128)


def make_update(triangle, gates, out_weight, tall):
    return pl.pallas_call(
        update_kernel,
        out_shape=jax.ShapeDtypeStruct((8, 4, 16, 128), BF16),
        scratch_shapes=[pltpu.VMEM((512, 128), F32)],
        compiler_params=params(),
        name="update",
    )(triangle, gates, out_weight, tall)


def order_kernel(place, update, out):
    own = place[0] // 8
    held = [PLACES[0][source] for source in range(8)]
    for target in range(1, 8):
        held = [
            jnp.where(own == target, PLACES[target][source], held[source]) for source in range(8)
        ]
    for block in range(4):
        even, odd = held[block * 2], held[block * 2 + 1]
        first = update[even].astype(F32).reshape(64, 128)
        second = update[odd].astype(F32).reshape(64, 128)
        upper, lower = cross_halves(first, second)
        lanes = slice(block * 128, block * 128 + 128)
        out[:4, :, lanes] = upper.astype(BF16).reshape(4, 16, 128)
        out[4:, :, lanes] = lower.astype(BF16).reshape(4, 16, 128)


def make_order(place, update):
    return pl.pallas_call(
        order_kernel,
        out_shape=jax.ShapeDtypeStruct((8, 16, 512), BF16),
        in_specs=[
            pl.BlockSpec(memory_space=pltpu.SMEM),
            pl.BlockSpec(memory_space=pltpu.VMEM),
        ],
        compiler_params=params(),
        name="order",
    )(place, update)


def exchange(values, axes):
    return lax.all_to_all(values, axes, 0, 0, tiled=True)


def shards(
    pair_rep,
    pair_gain,
    pair_bias,
    left_weight,
    right_weight,
    gate_weight,
    out_weight,
    out_gain,
    out_bias,
):
    swapped = [
        ((s * 8 + e) * 8 + t, (t * 8 + e) * 8 + PLACES[t][s])
        for s in range(8)
        for e in range(8)
        for t in range(8)
    ]
    place = lax.axis_index(AXES[:4]).astype(jnp.int32).reshape(1)
    edges, normed, tall = make_edges(
        pair_rep, pair_gain, pair_bias, left_weight, right_weight, out_gain, out_bias
    )
    moved = lax.ppermute(normed.reshape(8, 64, 128), AXES, swapped)
    edges = lax.cond(
        lax.axis_index("x") < 4,
        lambda held: exchange(held, SPLIT),
        lambda held: held,
        edges.reshape(64, 16, 128),
    )
    own = exchange(make_pack(edges, moved), "y")
    other = lax.ppermute(own, "co", [(0, 1), (1, 0)])
    triangle, gates = make_triangle(
        place, own, other, edges.reshape(8, 8, 16, 128), gate_weight
    )
    triangle = exchange(triangle.reshape(64, 8, 128), SPLIT)
    update = make_update(triangle, gates, out_weight, tall)
    return make_order(place, exchange(update, "n"))


def solution(mesh):
    fine = Mesh(mesh.devices.reshape(4, 2, 4, 2, 8), AXES)
    rows = ("x", "zh", "y", "co")
    in_specs = (P(rows, "n", None), P(), P(), P(), P(), P(), P(), P(), P())
    out_specs = P(rows, "n", None)
    return jax.shard_map(shards, mesh=fine, in_specs=in_specs, out_specs=out_specs, check_vma=False)
```

```python
import jax
import jax.numpy as jnp
from jax import lax
from jax.experimental import pallas as pl
from jax.experimental.pallas import tpu as pltpu
from jax.sharding import Mesh, PartitionSpec as P

F32 = jnp.float32
BF16 = jnp.bfloat16
ROWS = 8
AXES = ("x", "zh", "y", "co", "n")
SPLIT = ("n", "x", "zh")


PLACES = (
    (3, 4, 1, 5, 0, 7, 2, 6),
    (4, 3, 5, 0, 7, 1, 6, 2),
    (1, 5, 0, 4, 3, 6, 2, 7),
    (0, 2, 1, 5, 6, 4, 7, 3),
    (4, 0, 3, 1, 2, 6, 5, 7),
    (0, 5, 1, 4, 3, 7, 2, 6),
    (5, 1, 6, 0, 7, 2, 4, 3),
    (1, 5, 0, 7, 2, 6, 3, 4),
)


def params(mib=16):
    return pltpu.CompilerParams(vmem_limit_bytes=mib * 1024 * 1024)


def lane_mask(shape):
    return lax.broadcasted_iota(jnp.int32, shape, len(shape) - 1) < 64


def swap_halves(values):
    return pltpu.roll(values, 64, len(values.shape) - 1)


def cross_halves(first, second):
    low = lane_mask(first.shape)
    return (
        jnp.where(low, first, swap_halves(second)),
        jnp.where(low, swap_halves(first), second),
    )


def layer_norm(values, gain, bias):
    center = jnp.mean(values, axis=-1, keepdims=True)
    moved = values - center
    spread = jnp.mean(moved * moved, axis=-1, keepdims=True)
    return moved * lax.rsqrt(spread + 1e-05) * gain + bias


def edges_kernel(
    pair_hbm, gain_hbm, bias_hbm, left_hbm, right_hbm, last_gain_hbm, last_bias_hbm,
    edges, normed_hbm, tall_hbm, pair, gain, bias, left_weight, right_weight, last_gain, last_bias, scratch, normed, tall, sems,
):
    moves = [
        pltpu.make_async_copy(source, target, sems.at[slot])
        for slot, (source, target) in enumerate(
            (
                (pair_hbm, pair),
                (gain_hbm, gain),
                (bias_hbm, bias),
                (left_hbm, left_weight),
                (right_hbm, right_weight),
                (last_gain_hbm, last_gain),
                (last_bias_hbm, last_bias),
            )
        )
    ]
    for move in moves:
        move.start()
    for move in moves:
        move.wait()
    values = pair[...].astype(F32).reshape(512, 128)
    rounded = layer_norm(values, gain[...], bias[...]).astype(BF16)
    normed[...] = rounded
    tall[0] = jnp.transpose(jnp.broadcast_to(last_gain[...], (128, 128)))
    tall[1] = jnp.transpose(jnp.broadcast_to(last_bias[...], (128, 128)))
    results = [
        pltpu.make_async_copy(normed, normed_hbm, sems.at[7]),
        pltpu.make_async_copy(tall, tall_hbm, sems.at[8]),
    ]
    for result in results:
        result.start()
    for side, weight in enumerate((left_weight, right_weight)):
        both = lax.dot_general(
            weight[...], rounded, (((0,), (1,)), ((), ())), preferred_element_type=F32
        )
        edge = jax.nn.sigmoid(both[128:]) * both[:128]
        for block in range(4):
            lanes = slice(block * 128, block * 128 + 128)
            even, odd = cross_halves(edge[:64, lanes], edge[64:, lanes])
            start = side * 8 + block * 2
            scratch[pl.ds(start, 64, stride=16), :] = even
            scratch[pl.ds(start + 1, 64, stride=16), :] = odd
    edges[...] = scratch[...].astype(BF16)
    for result in results:
        result.wait()


def make_edges(pair, gain, bias, left_weight, right_weight, last_gain, last_bias):
    row = pltpu.VMEM((1, 128), F32)
    return pl.pallas_call(
        edges_kernel,
        out_shape=(
            jax.ShapeDtypeStruct((1024, 128), BF16),
            jax.ShapeDtypeStruct((512, 128), BF16),
            jax.ShapeDtypeStruct((2, 128, 128), F32),
        ),
        in_specs=[pl.BlockSpec(memory_space=pltpu.HBM)] * 7,
        out_specs=(
            pl.BlockSpec(memory_space=pltpu.VMEM),
            pl.BlockSpec(memory_space=pltpu.HBM),
            pl.BlockSpec(memory_space=pltpu.HBM),
        ),
        scratch_shapes=[
            pltpu.VMEM((8, 64, 128), BF16),
            row,
            row,
            pltpu.VMEM((128, 256), BF16),
            pltpu.VMEM((128, 256), BF16),
            row,
            row,
            pltpu.VMEM((1024, 128), F32),
            pltpu.VMEM((512, 128), BF16),
            pltpu.VMEM((2, 128, 128), F32),
            pltpu.SemaphoreType.DMA((9,)),
        ],
        compiler_params=params(63),
        name="edges",
    )(
        pair,
        gain.reshape(1, 128),
        bias.reshape(1, 128),
        left_weight,
        right_weight,
        last_gain.reshape(1, 128),
        last_bias.reshape(1, 128),
    )


def pack_kernel(edges, pair, payload):
    left = edges[:, :8].reshape(512, 128)
    for target in range(4):
        payload[target, :512] = left
        payload[target, 512:] = pair[:, target * 16 : target * 16 + 16].reshape(128, 128)


def make_pack(edges, pair):
    return pl.pallas_call(
        pack_kernel,
        out_shape=jax.ShapeDtypeStruct((4, 640, 128), BF16),
        compiler_params=params(),
        name="pack",
    )(edges, pair)


def triangle_kernel(
    place, own, other, edges, gate_weight, out, gates, normed
):
    first_core = place[0] % 2 == 0
    total = jnp.zeros((128, 512), F32)
    for part in range(8):
        rows = slice(part * 64, part * 64 + 64)
        mine = own[:, rows].astype(F32).reshape(4, 8, 8, 128)
        theirs = other[:, rows].astype(F32).reshape(4, 8, 8, 128)
        first = jnp.where(first_core, mine, theirs)
        second = jnp.where(first_core, theirs, mine)
        left = jnp.concatenate(
            [held[y, a] for a in range(8) for y in range(4) for held in (first, second)], axis=0
        ).astype(BF16)
        right = edges[part].astype(F32)[:, 8:].reshape(64, 128)
        low = lane_mask(right.shape)
        right = jnp.concatenate(
            [jnp.where(low, right, 0.0), jnp.where(low, 0.0, right)], axis=0
        ).astype(BF16)
        total += lax.dot_general(
            right, left, (((1,), (1,)), ((), ())), preferred_element_type=F32
        )
    shape = (64, 128)
    low = lane_mask(shape)
    upper = lax.broadcasted_iota(jnp.int32, shape, 0) % 8 < 4
    for block in range(4):
        columns = total[:, block * 128 : block * 128 + 128]
        turned = []
        for hidden in range(2):
            held = columns[hidden * 64 : hidden * 64 + 64]
            up, down = pltpu.roll(held, 60, 0), pltpu.roll(held, 4, 0)
            crossed = swap_halves(jnp.where(upper, up, down))
            turned.append(jnp.where(upper == low, held, crossed))
        even = jnp.where(upper, turned[0], pltpu.roll(turned[1], 4, 0))
        odd = jnp.where(upper, pltpu.roll(turned[0], 60, 0), turned[1])
        for side, rows in enumerate((even, odd)):
            rows = rows.astype(BF16).reshape(8, 8, 128)
            for target in range(8):
                out[PLACES[target][block * 2 + side], target] = rows[target]
    mine = own[:, 512:].astype(F32).reshape(32, 16, 128)
    theirs = other[:, 512:].astype(F32).reshape(32, 16, 128)
    mine = jnp.where(first_core, mine[:, :8], mine[:, 8:]).reshape(4, 64, 128)
    theirs = jnp.where(first_core, theirs[:, :8], theirs[:, 8:]).reshape(4, 64, 128)
    first = jnp.where(first_core, mine, theirs)
    second = jnp.where(first_core, theirs, mine)
    rows = jnp.concatenate([first, second], axis=1).reshape(512, 128)
    normed[...] = rows
    for part in range(4):
        rows = jnp.concatenate(
            [normed[pl.ds(part, 64, stride=8), :], normed[pl.ds(4 + part, 64, stride=8), :]],
            axis=0,
        ).astype(BF16)
        logits = lax.dot_general(
            gate_weight[...], rows, (((0,), (1,)), ((), ())), preferred_element_type=F32
        )
        gates[part] = jax.nn.sigmoid(logits)


def make_triangle(place, own, other, edges, gate_weight):
    return pl.pallas_call(
        triangle_kernel,
        out_shape=(
            jax.ShapeDtypeStruct((8, 8, 8, 128), BF16),
            jax.ShapeDtypeStruct((4, 128, 128), F32),
        ),
        in_specs=[pl.BlockSpec(memory_space=pltpu.SMEM)]
        + [pl.BlockSpec(memory_space=pltpu.VMEM)] * 4,
        scratch_shapes=[pltpu.VMEM((512, 128), F32)],
        compiler_params=params(),
        name="triangle",
    )(place, own, other, edges, gate_weight)


def update_kernel(triangle, gates, out_weight, tall, out, scratch):
    values = triangle[...].astype(F32)
    sums = jnp.sum(values, axis=0)
    squares = jnp.sum(values * values, axis=0)
    center = (sums + pltpu.roll(sums, 4, 0)) / 128
    spread = (squares + pltpu.roll(squares, 4, 0)) / 128 - center * center
    scale = lax.rsqrt(spread + 1e-05)
    scratch[...] = ((values - center) * scale).reshape(512, 128)
    for part in range(4):
        held = jnp.concatenate(
            [
                scratch[pl.ds(part, 64, stride=8), :],
                scratch[pl.ds(4 + part, 64, stride=8), :],
            ],
            axis=0,
        )
        held = (held * tall[0] + tall[1]).astype(BF16)
        projected = lax.dot_general(
            out_weight[...], held, (((0,), (0,)), ((), ())), preferred_element_type=F32
        )
        out[:, part] = (gates[part] * projected).astype(BF16).reshape(8, 16, 128)


def make_update(triangle, gates, out_weight, tall):
    return pl.pallas_call(
        update_kernel,
        out_shape=jax.ShapeDtypeStruct((8, 4, 16, 128), BF16),
        scratch_shapes=[pltpu.VMEM((512, 128), F32)],
        compiler_params=params(),
        name="update",
    )(triangle, gates, out_weight, tall)


def order_kernel(place, update, out):
    own = place[0] // 8
    held = [PLACES[0][source] for source in range(8)]
    for target in range(1, 8):
        held = [
            jnp.where(own == target, PLACES[target][source], held[source]) for source in range(8)
        ]
    for block in range(4):
        even, odd = held[block * 2], held[block * 2 + 1]
        first = update[even].astype(F32).reshape(64, 128)
        second = update[odd].astype(F32).reshape(64, 128)
        upper, lower = cross_halves(first, second)
        lanes = slice(block * 128, block * 128 + 128)
        out[:4, :, lanes] = upper.astype(BF16).reshape(4, 16, 128)
        out[4:, :, lanes] = lower.astype(BF16).reshape(4, 16, 128)


def make_order(place, update):
    return pl.pallas_call(
        order_kernel,
        out_shape=jax.ShapeDtypeStruct((8, 16, 512), BF16),
        in_specs=[
            pl.BlockSpec(memory_space=pltpu.SMEM),
            pl.BlockSpec(memory_space=pltpu.VMEM),
        ],
        compiler_params=params(),
        name="order",
    )(place, update)


def exchange(values, axes):
    return lax.all_to_all(values, axes, 0, 0, tiled=True)


def shards(
    pair_rep,
    pair_gain,
    pair_bias,
    left_weight,
    right_weight,
    gate_weight,
    out_weight,
    out_gain,
    out_bias,
):
    swapped = [
        ((s * 8 + e) * 8 + t, (t * 8 + e) * 8 + PLACES[t][s])
        for s in range(8)
        for e in range(8)
        for t in range(8)
    ]
    place = lax.axis_index(AXES[:4]).astype(jnp.int32).reshape(1)
    edges, normed, tall = make_edges(
        pair_rep, pair_gain, pair_bias, left_weight, right_weight, out_gain, out_bias
    )
    moved = lax.ppermute(normed.reshape(8, 64, 128), AXES, swapped)
    edges = lax.cond(
        lax.axis_index("x") < 4,
        lambda held: exchange(held, SPLIT),
        lambda held: held,
        edges.reshape(64, 16, 128),
    )
    own = exchange(make_pack(edges, moved), "y")
    other = lax.ppermute(own, "co", [(0, 1), (1, 0)])
    triangle, gates = make_triangle(
        place, own, other, edges.reshape(8, 8, 16, 128), gate_weight
    )
    triangle = exchange(triangle.reshape(64, 8, 128), SPLIT)
    update = make_update(triangle, gates, out_weight, tall)
    return make_order(place, exchange(update, "n"))


def solution(mesh):
    fine = Mesh(mesh.devices.reshape(4, 2, 4, 2, 8), AXES)
    rows = ("x", "zh", "y", "co")
    in_specs = (P(rows, "n", None), P(), P(), P(), P(), P(), P(), P(), P())
    out_specs = P(rows, "n", None)
    return jax.shard_map(shards, mesh=fine, in_specs=in_specs, out_specs=out_specs, check_vma=False)
```

```python
import jax
import jax.numpy as jnp
import numpy as np
from jax import lax
from jax.experimental import pallas as pl
from jax.experimental.pallas import tpu as pltpu
from jax.sharding import Mesh, PartitionSpec as P

F32 = jnp.float32
BF16 = jnp.bfloat16
ROWS = 8
AXES = ("x", "zh", "y", "co", "n")
SPLIT = ("n", "x", "zh")


PLACES = (
    (3, 4, 1, 5, 0, 7, 2, 6),
    (4, 3, 5, 0, 7, 1, 6, 2),
    (1, 5, 0, 4, 3, 6, 2, 7),
    (0, 2, 1, 5, 6, 4, 7, 3),
    (4, 0, 3, 1, 2, 6, 5, 7),
    (0, 5, 1, 4, 3, 7, 2, 6),
    (5, 1, 6, 0, 7, 2, 4, 3),
    (1, 5, 0, 7, 2, 6, 3, 4),
)


def params(mib=16):
    return pltpu.CompilerParams(vmem_limit_bytes=mib * 1024 * 1024)


def lane_mask(shape):
    return lax.broadcasted_iota(jnp.int32, shape, len(shape) - 1) < 64


def swap_halves(values):
    return pltpu.roll(values, 64, len(values.shape) - 1)


def cross_halves(first, second):
    low = lane_mask(first.shape)
    return (
        jnp.where(low, first, swap_halves(second)),
        jnp.where(low, swap_halves(first), second),
    )


def layer_norm(values, gain, bias):
    center = jnp.mean(values, axis=-1, keepdims=True)
    moved = values - center
    spread = jnp.mean(moved * moved, axis=-1, keepdims=True)
    return moved * lax.rsqrt(spread + 1e-05) * gain + bias


def edges_kernel(
    pair_hbm, gain_hbm, bias_hbm, left_hbm, right_hbm, last_gain_hbm, last_bias_hbm,
    edges, normed_hbm, tall_hbm, pair, gain, bias, left_weight, right_weight, last_gain, last_bias, scratch, normed, tall, sems,
):
    moves = [
        pltpu.make_async_copy(source, target, sems.at[slot])
        for slot, (source, target) in enumerate(
            (
                (pair_hbm, pair),
                (gain_hbm, gain),
                (bias_hbm, bias),
                (left_hbm, left_weight),
                (right_hbm, right_weight),
                (last_gain_hbm, last_gain),
                (last_bias_hbm, last_bias),
            )
        )
    ]
    for move in moves:
        move.start()
    for move in moves:
        move.wait()
    values = pair[...].astype(F32).reshape(512, 128)
    rounded = layer_norm(values, gain[...], bias[...]).astype(BF16)
    normed[...] = rounded
    tall[0] = jnp.transpose(jnp.broadcast_to(last_gain[...], (128, 128)))
    tall[1] = jnp.transpose(jnp.broadcast_to(last_bias[...], (128, 128)))
    results = [
        pltpu.make_async_copy(normed, normed_hbm, sems.at[7]),
        pltpu.make_async_copy(tall, tall_hbm, sems.at[8]),
    ]
    for result in results:
        result.start()
    for side, weight in enumerate((left_weight, right_weight)):
        both = lax.dot_general(
            weight[...], rounded, (((0,), (1,)), ((), ())), preferred_element_type=F32
        )
        edge = jax.nn.sigmoid(both[128:]) * both[:128]
        for block in range(4):
            lanes = slice(block * 128, block * 128 + 128)
            even, odd = cross_halves(edge[:64, lanes], edge[64:, lanes])
            start = side * 8 + block * 2
            scratch[pl.ds(start, 64, stride=16), :] = even
            scratch[pl.ds(start + 1, 64, stride=16), :] = odd
    edges[...] = scratch[...].astype(BF16)
    for result in results:
        result.wait()


def make_edges(pair, gain, bias, left_weight, right_weight, last_gain, last_bias):
    row = pltpu.VMEM((1, 128), F32)
    return pl.pallas_call(
        edges_kernel,
        out_shape=(
            jax.ShapeDtypeStruct((1024, 128), BF16),
            jax.ShapeDtypeStruct((512, 128), BF16),
            jax.ShapeDtypeStruct((2, 128, 128), F32),
        ),
        in_specs=[pl.BlockSpec(memory_space=pltpu.HBM)] * 7,
        out_specs=(
            pl.BlockSpec(memory_space=pltpu.VMEM),
            pl.BlockSpec(memory_space=pltpu.HBM),
            pl.BlockSpec(memory_space=pltpu.HBM),
        ),
        scratch_shapes=[
            pltpu.VMEM((8, 64, 128), BF16),
            row,
            row,
            pltpu.VMEM((128, 256), BF16),
            pltpu.VMEM((128, 256), BF16),
            row,
            row,
            pltpu.VMEM((1024, 128), F32),
            pltpu.VMEM((512, 128), BF16),
            pltpu.VMEM((2, 128, 128), F32),
            pltpu.SemaphoreType.DMA((9,)),
        ],
        compiler_params=params(63),
        name="edges",
    )(
        pair,
        gain.reshape(1, 128),
        bias.reshape(1, 128),
        left_weight,
        right_weight,
        last_gain.reshape(1, 128),
        last_bias.reshape(1, 128),
    )


def pack_kernel(edges, pair, payload, right):
    left = edges[:, :8].reshape(512, 128)
    for target in range(4):
        payload[target, :512] = left
        payload[target, 512:] = pair[:, target * 16 : target * 16 + 16].reshape(128, 128)
    right[...] = edges[:, 8:].reshape(512, 128)


def make_pack(edges, pair):
    return pl.pallas_call(
        pack_kernel,
        out_shape=(
            jax.ShapeDtypeStruct((4, 640, 128), BF16),
            jax.ShapeDtypeStruct((512, 128), BF16),
        ),
        compiler_params=params(),
        name="pack",
    )(edges, pair)


def triangle_kernel(place, received, right, other, gate_weight, out, gates, normed, rows):
    first_core = place[0] % 2 == 0
    total = jnp.zeros((256, 256), F32)
    for part in range(8):
        mine = right[part * 64 : part * 64 + 64].astype(F32)
        theirs = other[part * 64 : part * 64 + 64].astype(F32)
        low = lane_mask(mine.shape)
        sides = (jnp.where(first_core, mine, theirs), jnp.where(first_core, theirs, mine))
        halves = [jnp.where(low, side, 0.0) for side in sides]
        halves += [jnp.where(low, 0.0, side) for side in sides]
        right_rows = jnp.concatenate(
            [half[a * 8 : a * 8 + 8] for a in range(8) for half in halves], axis=0
        ).astype(BF16)
        held = received[:, part * 64 : part * 64 + 64].astype(F32)
        left_rows = jnp.concatenate(
            [held[y, a * 8 : a * 8 + 8] for a in range(8) for y in range(4)], axis=0
        ).astype(BF16)
        total += lax.dot_general(
            right_rows, left_rows, (((1,), (1,)), ((), ())), preferred_element_type=F32
        )
    lane_group = lax.broadcasted_iota(jnp.int32, (64, 128), 1) // 32
    for block in range(2):
        rows[block] = total[:, block * 128 : block * 128 + 128]
        taken = [rows[block, pl.ds(row, 64, stride=4), :] for row in range(4)]
        for group in range(4):
            turned = taken[0] if group == 0 else pltpu.roll(taken[0], 128 - group * 32, 1)
            for row in range(1, 4):
                shift = (row - group) * 32 % 128
                rolled = pltpu.roll(taken[row], shift, 1) if shift else taken[row]
                turned = jnp.where(lane_group == row, rolled, turned)
            turned = turned.astype(BF16).reshape(8, 8, 128)
            for target in range(8):
                out[PLACES[target][block * 4 + group], target] = turned[target]
    normed[...] = received[:, 512:].astype(F32).reshape(512, 128)
    for part in range(4):
        first = part // 2 * 8 + part % 2 * 4
        pairs = jnp.concatenate(
            [normed[pl.ds(first + row, 32, stride=16), :] for row in range(4)], axis=0
        ).astype(BF16)
        logits = lax.dot_general(
            gate_weight[...], pairs, (((0,), (1,)), ((), ())), preferred_element_type=F32
        )
        gates[part] = jax.nn.sigmoid(logits)


def make_triangle(place, received, right, other, gate_weight):
    return pl.pallas_call(
        triangle_kernel,
        out_shape=(
            jax.ShapeDtypeStruct((8, 8, 8, 128), BF16),
            jax.ShapeDtypeStruct((4, 128, 128), F32),
        ),
        in_specs=[pl.BlockSpec(memory_space=pltpu.SMEM)]
        + [pl.BlockSpec(memory_space=pltpu.VMEM)] * 4,
        scratch_shapes=[pltpu.VMEM((512, 128), F32), pltpu.VMEM((2, 256, 128), F32)],
        compiler_params=params(),
        name="triangle",
    )(place, received, right, other, gate_weight)


def update_kernel(triangle, gates, out_weight, tall, out, scratch):
    values = triangle[...].astype(F32)
    sums = jnp.sum(values, axis=0)
    squares = jnp.sum(values * values, axis=0)
    center = (sums + pltpu.roll(sums, 4, 0)) / 128
    spread = (squares + pltpu.roll(squares, 4, 0)) / 128 - center * center
    scale = lax.rsqrt(spread + 1e-05)
    scratch[...] = ((values - center) * scale).reshape(512, 128)
    for part in range(4):
        held = jnp.concatenate(
            [
                scratch[pl.ds(part, 64, stride=8), :],
                scratch[pl.ds(4 + part, 64, stride=8), :],
            ],
            axis=0,
        )
        held = (held * tall[0] + tall[1]).astype(BF16)
        projected = lax.dot_general(
            out_weight[...], held, (((0,), (0,)), ((), ())), preferred_element_type=F32
        )
        update = (gates[part] * projected).astype(BF16)
        out[part // 2, :, part % 2] = update.reshape(8, 16, 128)


def make_update(triangle, gates, out_weight, tall):
    return pl.pallas_call(
        update_kernel,
        out_shape=jax.ShapeDtypeStruct((2, 8, 2, 16, 128), BF16),
        scratch_shapes=[pltpu.VMEM((512, 128), F32)],
        compiler_params=params(),
        name="update",
    )(triangle, gates, out_weight, tall)


def order_matrix():
    lanes = np.arange(512).reshape(2, 2, 4, 4, 8).transpose(2, 0, 3, 1, 4).reshape(512)
    return (np.arange(512)[:, None] == lanes[None, :]).astype(jnp.bfloat16)


def order_kernel(place, update, matrix, out):
    own = place[0] // 8
    held = [PLACES[0][source] for source in range(8)]
    for target in range(1, 8):
        held = [
            jnp.where(own == target, PLACES[target][source], held[source]) for source in range(8)
        ]
    pieces = [
        jnp.concatenate(
            [update[core * 8 + held[block * 2 + side], half] for side in range(2) for core in range(2)],
            axis=1,
        )
        for block in range(4)
        for half in range(2)
    ]
    turned = jnp.dot(
        jnp.concatenate(pieces, axis=0), matrix[...], preferred_element_type=F32
    ).astype(BF16)
    for block in range(4):
        for half in range(2):
            rows = (block * 2 + half) * 16
            for row in range(4):
                out[half * 4 + row, :, block * 128 : block * 128 + 128] = turned[
                    rows : rows + 16, row * 128 : row * 128 + 128
                ]


def make_order(place, update):
    return pl.pallas_call(
        order_kernel,
        out_shape=jax.ShapeDtypeStruct((8, 16, 512), BF16),
        in_specs=[
            pl.BlockSpec(memory_space=pltpu.SMEM),
            pl.BlockSpec(memory_space=pltpu.VMEM),
            pl.BlockSpec(memory_space=pltpu.VMEM),
        ],
        compiler_params=params(),
        name="order",
    )(place, update, jnp.asarray(order_matrix()))


def exchange(values, axes):
    return lax.all_to_all(values, axes, 0, 0, tiled=True)


def shards(
    pair_rep,
    pair_gain,
    pair_bias,
    left_weight,
    right_weight,
    gate_weight,
    out_weight,
    out_gain,
    out_bias,
):
    swapped = [
        ((s * 8 + e) * 8 + t, (t * 8 + e) * 8 + PLACES[t][s])
        for s in range(8)
        for e in range(8)
        for t in range(8)
    ]
    place = lax.axis_index(AXES[:4]).astype(jnp.int32).reshape(1)
    edges, normed, tall = make_edges(
        pair_rep, pair_gain, pair_bias, left_weight, right_weight, out_gain, out_bias
    )
    moved = lax.ppermute(normed.reshape(8, 64, 128), AXES, swapped)
    edges = lax.cond(
        lax.axis_index("x") < 4,
        lambda held: exchange(held, SPLIT),
        lambda held: held,
        edges.reshape(64, 16, 128),
    )
    payload, right = make_pack(edges, moved)
    received = exchange(payload, "y")
    other = lax.ppermute(right, "co", [(0, 1), (1, 0)])
    triangle, gates = make_triangle(place, received, right, other, gate_weight)
    triangle = exchange(triangle.reshape(64, 8, 128), SPLIT)
    update = make_update(triangle, gates, out_weight, tall)
    return make_order(place, exchange(update.reshape(16, 2, 16, 128), ("co", "n")))


def solution(mesh):
    fine = Mesh(mesh.devices.reshape(4, 2, 4, 2, 8), AXES)
    rows = ("x", "zh", "y", "co")
    in_specs = (P(rows, "n", None), P(), P(), P(), P(), P(), P(), P(), P())
    out_specs = P(rows, "n", None)
    return jax.shard_map(shards, mesh=fine, in_specs=in_specs, out_specs=out_specs, check_vma=False)
```

```python
import jax
import jax.numpy as jnp
import numpy as np
from jax import lax
from jax.experimental import pallas as pl
from jax.experimental.pallas import tpu as pltpu
from jax.sharding import Mesh, PartitionSpec as P

F32 = jnp.float32
BF16 = jnp.bfloat16
ROWS = 8
AXES = ("x", "zh", "y", "co", "n")
SPLIT = ("n", "x", "zh")


PLACES = (
    (3, 4, 1, 5, 0, 7, 2, 6),
    (4, 3, 5, 0, 7, 1, 6, 2),
    (1, 5, 0, 4, 3, 6, 2, 7),
    (0, 2, 1, 5, 6, 4, 7, 3),
    (4, 0, 3, 1, 2, 6, 5, 7),
    (0, 5, 1, 4, 3, 7, 2, 6),
    (5, 1, 6, 0, 7, 2, 4, 3),
    (1, 5, 0, 7, 2, 6, 3, 4),
)


def params(mib=16):
    return pltpu.CompilerParams(vmem_limit_bytes=mib * 1024 * 1024)


def lane_mask(shape):
    return lax.broadcasted_iota(jnp.int32, shape, len(shape) - 1) < 64


def swap_halves(values):
    return pltpu.roll(values, 64, len(values.shape) - 1)


def cross_halves(first, second):
    low = lane_mask(first.shape)
    return (
        jnp.where(low, first, swap_halves(second)),
        jnp.where(low, swap_halves(first), second),
    )


def layer_norm(values, gain, bias):
    center = jnp.mean(values, axis=-1, keepdims=True)
    moved = values - center
    spread = jnp.mean(moved * moved, axis=-1, keepdims=True)
    return moved * lax.rsqrt(spread + 1e-05) * gain + bias


def edges_kernel(
    pair_hbm, gain_hbm, bias_hbm, left_hbm, right_hbm, last_gain_hbm, last_bias_hbm,
    edges, normed_hbm, tall_hbm, pair, gain, bias, left_weight, right_weight, last_gain, last_bias, scratch, normed, tall, sems,
):
    moves = [
        pltpu.make_async_copy(source, target, sems.at[slot])
        for slot, (source, target) in enumerate(
            (
                (pair_hbm, pair),
                (gain_hbm, gain),
                (bias_hbm, bias),
                (left_hbm, left_weight),
                (right_hbm, right_weight),
                (last_gain_hbm, last_gain),
                (last_bias_hbm, last_bias),
            )
        )
    ]
    for move in moves:
        move.start()
    for move in moves:
        move.wait()
    values = pair[...].astype(F32).reshape(512, 128)
    rounded = layer_norm(values, gain[...], bias[...]).astype(BF16)
    normed[...] = rounded
    tall[0] = jnp.transpose(jnp.broadcast_to(last_gain[...], (128, 128)))
    tall[1] = jnp.transpose(jnp.broadcast_to(last_bias[...], (128, 128)))
    results = [
        pltpu.make_async_copy(normed, normed_hbm, sems.at[7]),
        pltpu.make_async_copy(tall, tall_hbm, sems.at[8]),
    ]
    for result in results:
        result.start()
    for side, weight in enumerate((left_weight, right_weight)):
        both = lax.dot_general(
            weight[...], rounded, (((0,), (1,)), ((), ())), preferred_element_type=F32
        )
        edge = jax.nn.sigmoid(both[128:]) * both[:128]
        for block in range(4):
            lanes = slice(block * 128, block * 128 + 128)
            even, odd = cross_halves(edge[:64, lanes], edge[64:, lanes])
            start = side * 8 + block * 2
            scratch[pl.ds(start, 64, stride=16), :] = even
            scratch[pl.ds(start + 1, 64, stride=16), :] = odd
    edges[...] = scratch[:1024].astype(BF16)
    for result in results:
        result.wait()


def make_edges(pair, gain, bias, left_weight, right_weight, last_gain, last_bias):
    row = pltpu.VMEM((1, 128), F32)
    return pl.pallas_call(
        edges_kernel,
        out_shape=(
            jax.ShapeDtypeStruct((1024, 128), BF16),
            jax.ShapeDtypeStruct((512, 128), BF16),
            jax.ShapeDtypeStruct((2, 128, 128), F32),
        ),
        in_specs=[pl.BlockSpec(memory_space=pltpu.HBM)] * 7,
        out_specs=(
            pl.BlockSpec(memory_space=pltpu.VMEM),
            pl.BlockSpec(memory_space=pltpu.HBM),
            pl.BlockSpec(memory_space=pltpu.HBM),
        ),
        scratch_shapes=[
            pltpu.VMEM((8, 64, 128), BF16),
            row,
            row,
            pltpu.VMEM((128, 256), BF16),
            pltpu.VMEM((128, 256), BF16),
            row,
            row,
            pltpu.VMEM((1024 + 16, 128), F32),
            pltpu.VMEM((512, 128), BF16),
            pltpu.VMEM((2, 128, 128), F32),
            pltpu.SemaphoreType.DMA((9,)),
        ],
        compiler_params=params(63),
        name="edges",
    )(
        pair,
        gain.reshape(1, 128),
        bias.reshape(1, 128),
        left_weight,
        right_weight,
        last_gain.reshape(1, 128),
        last_bias.reshape(1, 128),
    )


def pack_kernel(edges, pair, payload, right):
    left = edges[:, :8].reshape(512, 128)
    for target in range(4):
        payload[target, :512] = left
        payload[target, 512:] = pair[:, target * 16 : target * 16 + 16].reshape(128, 128)
    right[...] = edges[:, 8:].reshape(512, 128)


def make_pack(edges, pair):
    return pl.pallas_call(
        pack_kernel,
        out_shape=(
            jax.ShapeDtypeStruct((4, 640, 128), BF16),
            jax.ShapeDtypeStruct((512, 128), BF16),
        ),
        compiler_params=params(),
        name="pack",
    )(edges, pair)


def triangle_kernel(place, received, right, other, gate_weight, out, gates, normed, rows):
    first_core = place[0] % 2 == 0
    total = jnp.zeros((256, 256), F32)
    for part in range(8):
        mine = right[part * 64 : part * 64 + 64].astype(F32)
        theirs = other[part * 64 : part * 64 + 64].astype(F32)
        low = lane_mask(mine.shape)
        sides = (jnp.where(first_core, mine, theirs), jnp.where(first_core, theirs, mine))
        halves = [jnp.where(low, side, 0.0) for side in sides]
        halves += [jnp.where(low, 0.0, side) for side in sides]
        right_rows = jnp.concatenate(
            [half[a * 8 : a * 8 + 8] for a in range(8) for half in halves], axis=0
        ).astype(BF16)
        held = received[:, part * 64 : part * 64 + 64].astype(F32)
        left_rows = jnp.concatenate(
            [held[y, a * 8 : a * 8 + 8] for a in range(8) for y in range(4)], axis=0
        ).astype(BF16)
        total += lax.dot_general(
            right_rows, left_rows, (((1,), (1,)), ((), ())), preferred_element_type=F32
        )
    lane_group = lax.broadcasted_iota(jnp.int32, (64, 128), 1) // 32
    for block in range(2):
        rows[block, :256] = total[:, block * 128 : block * 128 + 128]
        taken = [rows[block, pl.ds(row, 64, stride=4), :] for row in range(4)]
        for group in range(4):
            turned = taken[0] if group == 0 else pltpu.roll(taken[0], 128 - group * 32, 1)
            for row in range(1, 4):
                shift = (row - group) * 32 % 128
                rolled = pltpu.roll(taken[row], shift, 1) if shift else taken[row]
                turned = jnp.where(lane_group == row, rolled, turned)
            turned = turned.astype(BF16).reshape(8, 8, 128)
            for target in range(8):
                out[PLACES[target][block * 4 + group], target] = turned[target]
    normed[:512] = received[:, 512:].astype(F32).reshape(512, 128)
    for part in range(4):
        first = part // 2 * 8 + part % 2 * 4
        pairs = jnp.concatenate(
            [normed[pl.ds(first + row, 32, stride=16), :] for row in range(4)], axis=0
        ).astype(BF16)
        logits = lax.dot_general(
            gate_weight[...], pairs, (((0,), (1,)), ((), ())), preferred_element_type=F32
        )
        gates[part] = jax.nn.sigmoid(logits)


def make_triangle(place, received, right, other, gate_weight):
    return pl.pallas_call(
        triangle_kernel,
        out_shape=(
            jax.ShapeDtypeStruct((8, 8, 8, 128), BF16),
            jax.ShapeDtypeStruct((4, 128, 128), F32),
        ),
        in_specs=[pl.BlockSpec(memory_space=pltpu.SMEM)]
        + [pl.BlockSpec(memory_space=pltpu.VMEM)] * 4,
        scratch_shapes=[pltpu.VMEM((512 + 16, 128), F32), pltpu.VMEM((2, 256 + 8, 128), F32)],
        compiler_params=params(),
        name="triangle",
    )(place, received, right, other, gate_weight)


def update_kernel(triangle, gates, out_weight, tall, out, scratch):
    values = triangle[...].astype(F32)
    sums = jnp.sum(values, axis=0)
    squares = jnp.sum(values * values, axis=0)
    center = (sums + pltpu.roll(sums, 4, 0)) / 128
    spread = (squares + pltpu.roll(squares, 4, 0)) / 128 - center * center
    scale = lax.rsqrt(spread + 1e-05)
    scratch[:512] = ((values - center) * scale).reshape(512, 128)
    for part in range(4):
        held = jnp.concatenate(
            [
                scratch[pl.ds(part, 64, stride=8), :],
                scratch[pl.ds(4 + part, 64, stride=8), :],
            ],
            axis=0,
        )
        held = (held * tall[0] + tall[1]).astype(BF16)
        projected = lax.dot_general(
            out_weight[...], held, (((0,), (0,)), ((), ())), preferred_element_type=F32
        )
        update = (gates[part] * projected).astype(BF16)
        out[part // 2, :, part % 2] = update.reshape(8, 16, 128)


def make_update(triangle, gates, out_weight, tall):
    return pl.pallas_call(
        update_kernel,
        out_shape=jax.ShapeDtypeStruct((2, 8, 2, 16, 128), BF16),
        scratch_shapes=[pltpu.VMEM((512 + 8, 128), F32)],
        compiler_params=params(),
        name="update",
    )(triangle, gates, out_weight, tall)


def order_matrix():
    lanes = np.arange(512).reshape(2, 2, 4, 4, 8).transpose(2, 0, 3, 1, 4).reshape(512)
    return (np.arange(512)[:, None] == lanes[None, :]).astype(jnp.bfloat16)


def order_kernel(place, update, matrix, out):
    own = place[0] // 8
    held = [PLACES[0][source] for source in range(8)]
    for target in range(1, 8):
        held = [
            jnp.where(own == target, PLACES[target][source], held[source]) for source in range(8)
        ]
    pieces = [
        jnp.concatenate(
            [update[core * 8 + held[block * 2 + side], half] for side in range(2) for core in range(2)],
            axis=1,
        )
        for block in range(4)
        for half in range(2)
    ]
    turned = jnp.dot(
        jnp.concatenate(pieces, axis=0), matrix[...], preferred_element_type=F32
    ).astype(BF16)
    for block in range(4):
        for half in range(2):
            rows = (block * 2 + half) * 16
            for row in range(4):
                out[half * 4 + row, :, block * 128 : block * 128 + 128] = turned[
                    rows : rows + 16, row * 128 : row * 128 + 128
                ]


def make_order(place, update):
    return pl.pallas_call(
        order_kernel,
        out_shape=jax.ShapeDtypeStruct((8, 16, 512), BF16),
        in_specs=[
            pl.BlockSpec(memory_space=pltpu.SMEM),
            pl.BlockSpec(memory_space=pltpu.VMEM),
            pl.BlockSpec(memory_space=pltpu.VMEM),
        ],
        compiler_params=params(),
        name="order",
    )(place, update, jnp.asarray(order_matrix()))


def exchange(values, axes):
    return lax.all_to_all(values, axes, 0, 0, tiled=True)


def shards(
    pair_rep,
    pair_gain,
    pair_bias,
    left_weight,
    right_weight,
    gate_weight,
    out_weight,
    out_gain,
    out_bias,
):
    swapped = [
        ((s * 8 + e) * 8 + t, (t * 8 + e) * 8 + PLACES[t][s])
        for s in range(8)
        for e in range(8)
        for t in range(8)
    ]
    place = lax.axis_index(AXES[:4]).astype(jnp.int32).reshape(1)
    edges, normed, tall = make_edges(
        pair_rep, pair_gain, pair_bias, left_weight, right_weight, out_gain, out_bias
    )
    moved = lax.ppermute(normed.reshape(8, 64, 128), AXES, swapped)
    edges = lax.cond(
        lax.axis_index("x") < 4,
        lambda held: exchange(held, SPLIT),
        lambda held: held,
        edges.reshape(64, 16, 128),
    )
    payload, right = make_pack(edges, moved)
    received = exchange(payload, "y")
    other = lax.ppermute(right, "co", [(0, 1), (1, 0)])
    triangle, gates = make_triangle(place, received, right, other, gate_weight)
    triangle = exchange(triangle.reshape(64, 8, 128), SPLIT)
    update = make_update(triangle, gates, out_weight, tall)
    return make_order(place, exchange(update.reshape(16, 2, 16, 128), ("co", "n")))


def solution(mesh):
    fine = Mesh(mesh.devices.reshape(4, 2, 4, 2, 8), AXES)
    rows = ("x", "zh", "y", "co")
    in_specs = (P(rows, "n", None), P(), P(), P(), P(), P(), P(), P(), P())
    out_specs = P(rows, "n", None)
    return jax.shard_map(shards, mesh=fine, in_specs=in_specs, out_specs=out_specs, check_vma=False)
```

```python
import jax
import jax.numpy as jnp
import numpy as np
from jax import lax
from jax.experimental import pallas as pl
from jax.experimental.pallas import tpu as pltpu
from jax.sharding import Mesh, PartitionSpec as P

F32 = jnp.float32
BF16 = jnp.bfloat16
ROWS = 8
AXES = ("x", "zh", "y", "co", "n")
SPLIT = ("n", "x", "zh")


PLACES = (
    (3, 4, 1, 5, 0, 7, 2, 6),
    (4, 3, 5, 0, 7, 1, 6, 2),
    (1, 5, 0, 4, 3, 6, 2, 7),
    (0, 2, 1, 5, 6, 4, 7, 3),
    (4, 0, 3, 1, 2, 6, 5, 7),
    (0, 5, 1, 4, 3, 7, 2, 6),
    (5, 1, 6, 0, 7, 2, 4, 3),
    (1, 5, 0, 7, 2, 6, 3, 4),
)


def params(mib=16):
    return pltpu.CompilerParams(vmem_limit_bytes=mib * 1024 * 1024)


def lane_mask(shape):
    return lax.broadcasted_iota(jnp.int32, shape, len(shape) - 1) < 64


def swap_halves(values):
    return pltpu.roll(values, 64, len(values.shape) - 1)


def cross_halves(first, second):
    low = lane_mask(first.shape)
    return (
        jnp.where(low, first, swap_halves(second)),
        jnp.where(low, swap_halves(first), second),
    )


def layer_norm(values, gain, bias):
    center = jnp.mean(values, axis=-1, keepdims=True)
    moved = values - center
    spread = jnp.mean(moved * moved, axis=-1, keepdims=True)
    return moved * lax.rsqrt(spread + 1e-05) * gain + bias


def edges_kernel(
    pair_hbm, gain_hbm, bias_hbm, left_hbm, right_hbm, last_gain_hbm, last_bias_hbm,
    edges, normed_hbm, tall_hbm, pair, gain, bias, left_weight, right_weight, last_gain, last_bias, scratch, normed, tall, sems,
):
    moves = [
        pltpu.make_async_copy(source, target, sems.at[slot])
        for slot, (source, target) in enumerate(
            (
                (pair_hbm, pair),
                (gain_hbm, gain),
                (bias_hbm, bias),
                (left_hbm, left_weight),
                (right_hbm, right_weight),
                (last_gain_hbm, last_gain),
                (last_bias_hbm, last_bias),
            )
        )
    ]
    for move in moves:
        move.start()
    for move in moves:
        move.wait()
    values = pair[...].astype(F32).reshape(512, 128)
    rounded = layer_norm(values, gain[...], bias[...]).astype(BF16)
    normed[...] = rounded
    tall[0] = jnp.transpose(jnp.broadcast_to(last_gain[...], (128, 128)))
    tall[1] = jnp.transpose(jnp.broadcast_to(last_bias[...], (128, 128)))
    results = [
        pltpu.make_async_copy(normed, normed_hbm, sems.at[7]),
        pltpu.make_async_copy(tall, tall_hbm, sems.at[8]),
    ]
    for result in results:
        result.start()
    for side, weight in enumerate((left_weight, right_weight)):
        both = lax.dot_general(
            weight[...], rounded, (((0,), (1,)), ((), ())), preferred_element_type=F32
        )
        edge = jax.nn.sigmoid(both[128:]) * both[:128]
        for block in range(4):
            lanes = slice(block * 128, block * 128 + 128)
            even, odd = cross_halves(edge[:64, lanes], edge[64:, lanes])
            start = side * 8 + block * 2
            scratch[pl.ds(start, 64, stride=16), :] = even
            scratch[pl.ds(start + 1, 64, stride=16), :] = odd
    edges[...] = scratch[:1024].astype(BF16)
    for result in results:
        result.wait()


def make_edges(pair, gain, bias, left_weight, right_weight, last_gain, last_bias):
    row = pltpu.VMEM((1, 128), F32)
    return pl.pallas_call(
        edges_kernel,
        out_shape=(
            jax.ShapeDtypeStruct((1024, 128), BF16),
            jax.ShapeDtypeStruct((512, 128), BF16),
            jax.ShapeDtypeStruct((2, 128, 128), F32),
        ),
        in_specs=[pl.BlockSpec(memory_space=pltpu.HBM)] * 7,
        out_specs=(
            pl.BlockSpec(memory_space=pltpu.VMEM),
            pl.BlockSpec(memory_space=pltpu.HBM),
            pl.BlockSpec(memory_space=pltpu.HBM),
        ),
        scratch_shapes=[
            pltpu.VMEM((8, 64, 128), BF16),
            row,
            row,
            pltpu.VMEM((128, 256), BF16),
            pltpu.VMEM((128, 256), BF16),
            row,
            row,
            pltpu.VMEM((1024 + 16, 128), F32),
            pltpu.VMEM((512, 128), BF16),
            pltpu.VMEM((2, 128, 128), F32),
            pltpu.SemaphoreType.DMA((9,)),
        ],
        compiler_params=params(63),
        name="edges",
    )(
        pair,
        gain.reshape(1, 128),
        bias.reshape(1, 128),
        left_weight,
        right_weight,
        last_gain.reshape(1, 128),
        last_bias.reshape(1, 128),
    )


def pack_kernel(edges, pair, payload, right):
    left = edges[:, :8].reshape(512, 128)
    for target in range(4):
        payload[target, :512] = left
        payload[target, 512:] = pair[:, target * 16 : target * 16 + 16].reshape(128, 128)
    right[...] = edges[:, 8:].reshape(512, 128)


def make_pack(edges, pair):
    return pl.pallas_call(
        pack_kernel,
        out_shape=(
            jax.ShapeDtypeStruct((4, 640, 128), BF16),
            jax.ShapeDtypeStruct((512, 128), BF16),
        ),
        compiler_params=params(),
        name="pack",
    )(edges, pair)


def triangle_kernel(place, received, right, other, gate_weight, out, gates, normed, rows):
    first_core = place[0] % 2 == 0
    total = jnp.zeros((256, 256), F32)
    for part in range(8):
        mine = right[part * 64 : part * 64 + 64].astype(F32)
        theirs = other[part * 64 : part * 64 + 64].astype(F32)
        low = lane_mask(mine.shape)
        sides = (jnp.where(first_core, mine, theirs), jnp.where(first_core, theirs, mine))
        halves = [jnp.where(low, side, 0.0) for side in sides]
        halves += [jnp.where(low, 0.0, side) for side in sides]
        right_rows = jnp.concatenate(
            [half[a * 8 : a * 8 + 8] for a in range(8) for half in halves], axis=0
        ).astype(BF16)
        held = received[:, part * 64 : part * 64 + 64].astype(F32)
        left_rows = jnp.concatenate(
            [held[y, a * 8 : a * 8 + 8] for a in range(8) for y in range(4)], axis=0
        ).astype(BF16)
        total += lax.dot_general(
            right_rows, left_rows, (((1,), (1,)), ((), ())), preferred_element_type=F32
        )
    lane_group = lax.broadcasted_iota(jnp.int32, (64, 128), 1) // 32
    for block in range(2):
        rows[block, :256] = total[:, block * 128 : block * 128 + 128]
        taken = [rows[block, pl.ds(row, 64, stride=4), :] for row in range(4)]
        for group in range(4):
            turned = taken[0] if group == 0 else pltpu.roll(taken[0], 128 - group * 32, 1)
            for row in range(1, 4):
                shift = (row - group) * 32 % 128
                rolled = pltpu.roll(taken[row], shift, 1) if shift else taken[row]
                turned = jnp.where(lane_group == row, rolled, turned)
            turned = turned.astype(BF16).reshape(8, 8, 128)
            for target in range(8):
                out[PLACES[target][block * 4 + group], target] = turned[target]
    normed[:512] = received[:, 512:].astype(F32).reshape(512, 128)
    for part in range(4):
        first = part // 2 * 8 + part % 2 * 4
        pairs = jnp.concatenate(
            [normed[pl.ds(first + row, 32, stride=16), :] for row in range(4)], axis=0
        ).astype(BF16)
        logits = lax.dot_general(
            gate_weight[...], pairs, (((0,), (1,)), ((), ())), preferred_element_type=F32
        )
        gates[part] = jax.nn.sigmoid(logits)


def make_triangle(place, received, right, other, gate_weight):
    return pl.pallas_call(
        triangle_kernel,
        out_shape=(
            jax.ShapeDtypeStruct((8, 8, 8, 128), BF16),
            jax.ShapeDtypeStruct((4, 128, 128), F32),
        ),
        in_specs=[pl.BlockSpec(memory_space=pltpu.SMEM)]
        + [pl.BlockSpec(memory_space=pltpu.VMEM)] * 4,
        scratch_shapes=[pltpu.VMEM((512 + 16, 128), F32), pltpu.VMEM((2, 256 + 8, 128), F32)],
        compiler_params=params(),
        name="triangle",
    )(place, received, right, other, gate_weight)


def update_kernel(triangle, gates, out_weight, tall, out, scratch):
    values = triangle[...].astype(F32)
    sums = jnp.sum(values, axis=0)
    squares = jnp.sum(values * values, axis=0)
    center = (sums + pltpu.roll(sums, 4, 0)) / 128
    spread = (squares + pltpu.roll(squares, 4, 0)) / 128 - center * center
    scale = lax.rsqrt(spread + 1e-05)
    scratch[:512] = ((values - center) * scale).reshape(512, 128)
    for part in range(4):
        held = jnp.concatenate(
            [
                scratch[pl.ds(part, 64, stride=8), :],
                scratch[pl.ds(4 + part, 64, stride=8), :],
            ],
            axis=0,
        )
        held = (held * tall[0] + tall[1]).astype(BF16)
        projected = lax.dot_general(
            out_weight[...], held, (((0,), (0,)), ((), ())), preferred_element_type=F32
        )
        update = (gates[part] * projected).astype(BF16)
        out[:, part // 2, part % 2] = update.reshape(8, 16, 128)


def make_update(triangle, gates, out_weight, tall):
    return pl.pallas_call(
        update_kernel,
        out_shape=jax.ShapeDtypeStruct((8, 2, 2, 16, 128), BF16),
        scratch_shapes=[pltpu.VMEM((512 + 8, 128), F32)],
        compiler_params=params(),
        name="update",
    )(triangle, gates, out_weight, tall)


def order_matrix():
    lanes = np.arange(512).reshape(2, 2, 4, 4, 8).transpose(2, 0, 3, 1, 4).reshape(512)
    return (np.arange(512)[:, None] == lanes[None, :]).astype(jnp.bfloat16)


def order_kernel(place, update, matrix, out):
    own = place[0] // 8
    held = [PLACES[0][source] for source in range(8)]
    for target in range(1, 8):
        held = [
            jnp.where(own == target, PLACES[target][source], held[source]) for source in range(8)
        ]
    pieces = [
        jnp.concatenate(
            [update[held[block * 2 + side] * 2 + core, half] for side in range(2) for core in range(2)],
            axis=1,
        )
        for block in range(4)
        for half in range(2)
    ]
    turned = jnp.dot(
        jnp.concatenate(pieces, axis=0), matrix[...], preferred_element_type=F32
    ).astype(BF16)
    for block in range(4):
        for half in range(2):
            rows = (block * 2 + half) * 16
            for row in range(4):
                out[half * 4 + row, :, block * 128 : block * 128 + 128] = turned[
                    rows : rows + 16, row * 128 : row * 128 + 128
                ]


def make_order(place, update):
    return pl.pallas_call(
        order_kernel,
        out_shape=jax.ShapeDtypeStruct((8, 16, 512), BF16),
        in_specs=[
            pl.BlockSpec(memory_space=pltpu.SMEM),
            pl.BlockSpec(memory_space=pltpu.VMEM),
            pl.BlockSpec(memory_space=pltpu.VMEM),
        ],
        compiler_params=params(),
        name="order",
    )(place, update, jnp.asarray(order_matrix()))


def exchange(values, axes):
    return lax.all_to_all(values, axes, 0, 0, tiled=True)


def shards(
    pair_rep,
    pair_gain,
    pair_bias,
    left_weight,
    right_weight,
    gate_weight,
    out_weight,
    out_gain,
    out_bias,
):
    swapped = [
        ((s * 8 + e) * 8 + t, (t * 8 + e) * 8 + PLACES[t][s])
        for s in range(8)
        for e in range(8)
        for t in range(8)
    ]
    place = lax.axis_index(AXES[:4]).astype(jnp.int32).reshape(1)
    edges, normed, tall = make_edges(
        pair_rep, pair_gain, pair_bias, left_weight, right_weight, out_gain, out_bias
    )
    moved = lax.ppermute(normed.reshape(8, 64, 128), AXES, swapped)
    edges = lax.cond(
        lax.axis_index("x") < 4,
        lambda held: exchange(held, SPLIT),
        lambda held: held,
        edges.reshape(64, 16, 128),
    )
    payload, right = make_pack(edges, moved)
    received = exchange(payload, "y")
    other = lax.ppermute(right, "co", [(0, 1), (1, 0)])
    triangle, gates = make_triangle(place, received, right, other, gate_weight)
    triangle = exchange(triangle.reshape(64, 8, 128), SPLIT)
    update = make_update(triangle, gates, out_weight, tall)
    return make_order(place, exchange(update.reshape(16, 2, 16, 128), ("n", "co")))


def solution(mesh):
    fine = Mesh(mesh.devices.reshape(4, 2, 4, 2, 8), AXES)
    rows = ("x", "zh", "y", "co")
    in_specs = (P(rows, "n", None), P(), P(), P(), P(), P(), P(), P(), P())
    out_specs = P(rows, "n", None)
    return jax.shard_map(shards, mesh=fine, in_specs=in_specs, out_specs=out_specs, check_vma=False)
```

```python
import jax
import jax.numpy as jnp
import numpy as np
from jax import lax
from jax.experimental import pallas as pl
from jax.experimental.pallas import tpu as pltpu
from jax.sharding import Mesh, PartitionSpec as P

F32 = jnp.float32
BF16 = jnp.bfloat16
ROWS = 8
AXES = ("x", "zh", "y", "co", "n")
SPLIT = ("n", "x", "zh")


PLACES = (
    (3, 4, 1, 5, 0, 7, 2, 6),
    (4, 3, 5, 0, 7, 1, 6, 2),
    (1, 5, 0, 4, 3, 6, 2, 7),
    (0, 2, 1, 5, 6, 4, 7, 3),
    (4, 0, 3, 1, 2, 6, 5, 7),
    (0, 5, 1, 4, 3, 7, 2, 6),
    (5, 1, 6, 0, 7, 2, 4, 3),
    (1, 5, 0, 7, 2, 6, 3, 4),
)


def params(mib=16):
    return pltpu.CompilerParams(vmem_limit_bytes=mib * 1024 * 1024)


def lane_mask(shape):
    return lax.broadcasted_iota(jnp.int32, shape, len(shape) - 1) < 64


def swap_halves(values):
    return pltpu.roll(values, 64, len(values.shape) - 1)


def cross_halves(first, second):
    low = lane_mask(first.shape)
    return (
        jnp.where(low, first, swap_halves(second)),
        jnp.where(low, swap_halves(first), second),
    )


def layer_norm(values, gain, bias):
    center = jnp.mean(values, axis=-1, keepdims=True)
    moved = values - center
    spread = jnp.mean(moved * moved, axis=-1, keepdims=True)
    return moved * lax.rsqrt(spread + 1e-05) * gain + bias


def edges_kernel(
    pair_hbm, gain_hbm, bias_hbm, left_hbm, right_hbm, last_gain_hbm, last_bias_hbm,
    edges, normed_hbm, tall_hbm, pair, gain, bias, left_weight, right_weight, last_gain, last_bias, scratch, normed, tall, sems,
):
    moves = [
        pltpu.make_async_copy(source, target, sems.at[slot])
        for slot, (source, target) in enumerate(
            (
                (pair_hbm, pair),
                (gain_hbm, gain),
                (bias_hbm, bias),
                (left_hbm, left_weight),
                (right_hbm, right_weight),
                (last_gain_hbm, last_gain),
                (last_bias_hbm, last_bias),
            )
        )
    ]
    for move in moves:
        move.start()
    for move in moves:
        move.wait()
    values = pair[...].astype(F32).reshape(512, 128)
    rounded = layer_norm(values, gain[...], bias[...]).astype(BF16)
    normed[...] = rounded
    tall[0] = jnp.transpose(jnp.broadcast_to(last_gain[...], (128, 128)))
    tall[1] = jnp.transpose(jnp.broadcast_to(last_bias[...], (128, 128)))
    results = [
        pltpu.make_async_copy(normed, normed_hbm, sems.at[7]),
        pltpu.make_async_copy(tall, tall_hbm, sems.at[8]),
    ]
    for result in results:
        result.start()
    for side, weight in enumerate((left_weight, right_weight)):
        both = lax.dot_general(
            weight[...], rounded, (((0,), (1,)), ((), ())), preferred_element_type=F32
        )
        edge = jax.nn.sigmoid(both[128:]) * both[:128]
        for block in range(4):
            lanes = slice(block * 128, block * 128 + 128)
            even, odd = cross_halves(edge[:64, lanes], edge[64:, lanes])
            start = side * 8 + block * 2
            scratch[pl.ds(start, 64, stride=16), :] = even
            scratch[pl.ds(start + 1, 64, stride=16), :] = odd
    edges[...] = scratch[:1024].astype(BF16)
    for result in results:
        result.wait()


def make_edges(pair, gain, bias, left_weight, right_weight, last_gain, last_bias):
    row = pltpu.VMEM((1, 128), F32)
    return pl.pallas_call(
        edges_kernel,
        out_shape=(
            jax.ShapeDtypeStruct((1024, 128), BF16),
            jax.ShapeDtypeStruct((512, 128), BF16),
            jax.ShapeDtypeStruct((2, 128, 128), F32),
        ),
        in_specs=[pl.BlockSpec(memory_space=pltpu.HBM)] * 7,
        out_specs=(
            pl.BlockSpec(memory_space=pltpu.VMEM),
            pl.BlockSpec(memory_space=pltpu.HBM),
            pl.BlockSpec(memory_space=pltpu.HBM),
        ),
        scratch_shapes=[
            pltpu.VMEM((8, 64, 128), BF16),
            row,
            row,
            pltpu.VMEM((128, 256), BF16),
            pltpu.VMEM((128, 256), BF16),
            row,
            row,
            pltpu.VMEM((1024 + 16, 128), F32),
            pltpu.VMEM((512, 128), BF16),
            pltpu.VMEM((2, 128, 128), F32),
            pltpu.SemaphoreType.DMA((9,)),
        ],
        compiler_params=params(63),
        name="edges",
    )(
        pair,
        gain.reshape(1, 128),
        bias.reshape(1, 128),
        left_weight,
        right_weight,
        last_gain.reshape(1, 128),
        last_bias.reshape(1, 128),
    )


def pack_kernel(edges, pair, payload):
    left = edges[:, :8].reshape(512, 128)
    for target in range(4):
        payload[target, :512] = left
        payload[target, 512:] = pair[:, target * 16 : target * 16 + 16].reshape(128, 128)


def make_pack(edges, pair):
    return pl.pallas_call(
        pack_kernel,
        out_shape=jax.ShapeDtypeStruct((4, 640, 128), BF16),
        compiler_params=params(),
        name="pack",
    )(edges, pair)


def triangle_kernel(place, received, right, other, gate_weight, out, gates, normed, rows):
    first_core = place[0] % 2 == 0
    total = jnp.zeros((256, 256), F32)
    for part in range(8):
        mine = right[part * 64 : part * 64 + 64].astype(F32)
        theirs = other[part * 64 : part * 64 + 64].astype(F32)
        low = lane_mask(mine.shape)
        sides = (jnp.where(first_core, mine, theirs), jnp.where(first_core, theirs, mine))
        halves = [jnp.where(low, side, 0.0) for side in sides]
        halves += [jnp.where(low, 0.0, side) for side in sides]
        right_rows = jnp.concatenate(
            [half[a * 8 : a * 8 + 8] for a in range(8) for half in halves], axis=0
        ).astype(BF16)
        held = received[:, part * 64 : part * 64 + 64].astype(F32)
        left_rows = jnp.concatenate(
            [held[y, a * 8 : a * 8 + 8] for a in range(8) for y in range(4)], axis=0
        ).astype(BF16)
        total += lax.dot_general(
            right_rows, left_rows, (((1,), (1,)), ((), ())), preferred_element_type=F32
        )
    lane_group = lax.broadcasted_iota(jnp.int32, (64, 128), 1) // 32
    for block in range(2):
        rows[block, :256] = total[:, block * 128 : block * 128 + 128]
        taken = [rows[block, pl.ds(row, 64, stride=4), :] for row in range(4)]
        for group in range(4):
            turned = taken[0] if group == 0 else pltpu.roll(taken[0], 128 - group * 32, 1)
            for row in range(1, 4):
                shift = (row - group) * 32 % 128
                rolled = pltpu.roll(taken[row], shift, 1) if shift else taken[row]
                turned = jnp.where(lane_group == row, rolled, turned)
            turned = turned.astype(BF16).reshape(8, 8, 128)
            for target in range(8):
                out[PLACES[target][block * 4 + group], target] = turned[target]
    normed[:512] = received[:, 512:].astype(F32).reshape(512, 128)
    for part in range(4):
        first = part // 2 * 8 + part % 2 * 4
        pairs = jnp.concatenate(
            [normed[pl.ds(first + row, 32, stride=16), :] for row in range(4)], axis=0
        ).astype(BF16)
        logits = lax.dot_general(
            gate_weight[...], pairs, (((0,), (1,)), ((), ())), preferred_element_type=F32
        )
        gates[part] = jax.nn.sigmoid(logits)


def make_triangle(place, received, right, other, gate_weight):
    return pl.pallas_call(
        triangle_kernel,
        out_shape=(
            jax.ShapeDtypeStruct((8, 8, 8, 128), BF16),
            jax.ShapeDtypeStruct((4, 128, 128), F32),
        ),
        in_specs=[pl.BlockSpec(memory_space=pltpu.SMEM)]
        + [pl.BlockSpec(memory_space=pltpu.VMEM)] * 4,
        scratch_shapes=[pltpu.VMEM((512 + 16, 128), F32), pltpu.VMEM((2, 256 + 8, 128), F32)],
        compiler_params=params(),
        name="triangle",
    )(place, received, right, other, gate_weight)


def update_kernel(triangle, gates, out_weight, tall, out, scratch):
    values = triangle[...].astype(F32)
    sums = jnp.sum(values, axis=0)
    squares = jnp.sum(values * values, axis=0)
    center = (sums + pltpu.roll(sums, 4, 0)) / 128
    spread = (squares + pltpu.roll(squares, 4, 0)) / 128 - center * center
    scale = lax.rsqrt(spread + 1e-05)
    scratch[:512] = ((values - center) * scale).reshape(512, 128)
    for part in range(4):
        held = jnp.concatenate(
            [
                scratch[pl.ds(part, 64, stride=8), :],
                scratch[pl.ds(4 + part, 64, stride=8), :],
            ],
            axis=0,
        )
        held = (held * tall[0] + tall[1]).astype(BF16)
        projected = lax.dot_general(
            out_weight[...], held, (((0,), (0,)), ((), ())), preferred_element_type=F32
        )
        update = (gates[part] * projected).astype(BF16)
        out[:, part // 2, part % 2] = update.reshape(8, 16, 128)


def make_update(triangle, gates, out_weight, tall):
    return pl.pallas_call(
        update_kernel,
        out_shape=jax.ShapeDtypeStruct((8, 2, 2, 16, 128), BF16),
        scratch_shapes=[pltpu.VMEM((512 + 8, 128), F32)],
        compiler_params=params(),
        name="update",
    )(triangle, gates, out_weight, tall)


def order_matrix():
    lanes = np.arange(512).reshape(2, 2, 4, 4, 8).transpose(2, 0, 3, 1, 4).reshape(512)
    return (np.arange(512)[:, None] == lanes[None, :]).astype(jnp.bfloat16)


def order_kernel(place, update, matrix, out):
    own = place[0] // 8
    held = [PLACES[0][source] for source in range(8)]
    for target in range(1, 8):
        held = [
            jnp.where(own == target, PLACES[target][source], held[source]) for source in range(8)
        ]
    pieces = [
        jnp.concatenate(
            [update[held[block * 2 + side] * 2 + core, half] for side in range(2) for core in range(2)],
            axis=1,
        )
        for block in range(4)
        for half in range(2)
    ]
    turned = jnp.dot(
        jnp.concatenate(pieces, axis=0), matrix[...], preferred_element_type=F32
    ).astype(BF16)
    for block in range(4):
        for half in range(2):
            rows = (block * 2 + half) * 16
            for row in range(4):
                out[half * 4 + row, :, block * 128 : block * 128 + 128] = turned[
                    rows : rows + 16, row * 128 : row * 128 + 128
                ]


def make_order(place, update):
    return pl.pallas_call(
        order_kernel,
        out_shape=jax.ShapeDtypeStruct((8, 16, 512), BF16),
        in_specs=[
            pl.BlockSpec(memory_space=pltpu.SMEM),
            pl.BlockSpec(memory_space=pltpu.VMEM),
            pl.BlockSpec(memory_space=pltpu.VMEM),
        ],
        compiler_params=params(),
        name="order",
    )(place, update, jnp.asarray(order_matrix()))


def exchange(values, axes):
    return lax.all_to_all(values, axes, 0, 0, tiled=True)


def shards(
    pair_rep,
    pair_gain,
    pair_bias,
    left_weight,
    right_weight,
    gate_weight,
    out_weight,
    out_gain,
    out_bias,
):
    swapped = [
        ((s * 8 + e) * 8 + t, (t * 8 + e) * 8 + PLACES[t][s])
        for s in range(8)
        for e in range(8)
        for t in range(8)
    ]
    place = lax.axis_index(AXES[:4]).astype(jnp.int32).reshape(1)
    edges, normed, tall = make_edges(
        pair_rep, pair_gain, pair_bias, left_weight, right_weight, out_gain, out_bias
    )
    moved = lax.ppermute(normed.reshape(8, 64, 128), AXES, swapped)
    edges = lax.cond(
        lax.axis_index("x") < 4,
        lambda held: exchange(held, SPLIT),
        lambda held: held,
        edges.reshape(64, 16, 128),
    )
    received = exchange(make_pack(edges, moved), "y")
    right = edges[:, 8:].reshape(512, 128)
    other = lax.ppermute(right, "co", [(0, 1), (1, 0)])
    triangle, gates = make_triangle(place, received, right, other, gate_weight)
    triangle = exchange(triangle.reshape(64, 8, 128), SPLIT)
    update = make_update(triangle, gates, out_weight, tall)
    return make_order(place, exchange(update.reshape(16, 2, 16, 128), ("n", "co")))


def solution(mesh):
    fine = Mesh(mesh.devices.reshape(4, 2, 4, 2, 8), AXES)
    rows = ("x", "zh", "y", "co")
    in_specs = (P(rows, "n", None), P(), P(), P(), P(), P(), P(), P(), P())
    out_specs = P(rows, "n", None)
    return jax.shard_map(shards, mesh=fine, in_specs=in_specs, out_specs=out_specs, check_vma=False)
```

```python
import jax
import jax.numpy as jnp
import numpy as np
from jax import lax
from jax.experimental import pallas as pl
from jax.experimental.pallas import tpu as pltpu
from jax.sharding import Mesh, PartitionSpec as P

F32 = jnp.float32
BF16 = jnp.bfloat16
ROWS = 8
AXES = ("x", "zh", "y", "co", "n")
SPLIT = ("n", "x", "zh")


PLACES = (
    (3, 4, 1, 5, 0, 7, 2, 6),
    (4, 3, 5, 0, 7, 1, 6, 2),
    (1, 5, 0, 4, 3, 6, 2, 7),
    (0, 2, 1, 5, 6, 4, 7, 3),
    (4, 0, 3, 1, 2, 6, 5, 7),
    (0, 5, 1, 4, 3, 7, 2, 6),
    (5, 1, 6, 0, 7, 2, 4, 3),
    (1, 5, 0, 7, 2, 6, 3, 4),
)


def params(mib=16):
    return pltpu.CompilerParams(vmem_limit_bytes=mib * 1024 * 1024)


def lane_mask(shape):
    return lax.broadcasted_iota(jnp.int32, shape, len(shape) - 1) < 64


def swap_halves(values):
    return pltpu.roll(values, 64, len(values.shape) - 1)


def cross_halves(first, second):
    low = lane_mask(first.shape)
    return (
        jnp.where(low, first, swap_halves(second)),
        jnp.where(low, swap_halves(first), second),
    )


def layer_norm(values, gain, bias):
    center = jnp.mean(values, axis=-1, keepdims=True)
    moved = values - center
    spread = jnp.mean(moved * moved, axis=-1, keepdims=True)
    return moved * lax.rsqrt(spread + 1e-05) * gain + bias


def edges_kernel(
    pair_hbm, gain_hbm, bias_hbm, left_hbm, right_hbm, last_gain_hbm, last_bias_hbm,
    edges, normed_hbm, tall_hbm, pair, gain, bias, left_weight, right_weight, last_gain, last_bias, scratch, normed, tall, sems,
):
    moves = [
        pltpu.make_async_copy(source, target, sems.at[slot])
        for slot, (source, target) in enumerate(
            (
                (pair_hbm, pair),
                (gain_hbm, gain),
                (bias_hbm, bias),
                (left_hbm, left_weight),
                (right_hbm, right_weight),
                (last_gain_hbm, last_gain),
                (last_bias_hbm, last_bias),
            )
        )
    ]
    for move in moves:
        move.start()
    for move in moves:
        move.wait()
    values = pair[...].astype(F32).reshape(512, 128)
    rounded = layer_norm(values, gain[...], bias[...]).astype(BF16)
    normed[...] = rounded
    tall[0] = jnp.transpose(jnp.broadcast_to(last_gain[...], (128, 128)))
    tall[1] = jnp.transpose(jnp.broadcast_to(last_bias[...], (128, 128)))
    results = [
        pltpu.make_async_copy(normed, normed_hbm, sems.at[7]),
        pltpu.make_async_copy(tall, tall_hbm, sems.at[8]),
    ]
    for result in results:
        result.start()
    for side, weight in enumerate((left_weight, right_weight)):
        both = lax.dot_general(
            weight[...], rounded, (((0,), (1,)), ((), ())), preferred_element_type=F32
        )
        edge = (0.5 * jnp.tanh(0.5 * both[128:]) + 0.5) * both[:128]
        for block in range(4):
            lanes = slice(block * 128, block * 128 + 128)
            even, odd = cross_halves(edge[:64, lanes], edge[64:, lanes])
            start = side * 8 + block * 2
            scratch[pl.ds(start, 64, stride=16), :] = even
            scratch[pl.ds(start + 1, 64, stride=16), :] = odd
    edges[...] = scratch[:1024].astype(BF16)
    for result in results:
        result.wait()


def make_edges(pair, gain, bias, left_weight, right_weight, last_gain, last_bias):
    row = pltpu.VMEM((1, 128), F32)
    return pl.pallas_call(
        edges_kernel,
        out_shape=(
            jax.ShapeDtypeStruct((1024, 128), BF16),
            jax.ShapeDtypeStruct((512, 128), BF16),
            jax.ShapeDtypeStruct((2, 128, 128), F32),
        ),
        in_specs=[pl.BlockSpec(memory_space=pltpu.HBM)] * 7,
        out_specs=(
            pl.BlockSpec(memory_space=pltpu.VMEM),
            pl.BlockSpec(memory_space=pltpu.HBM),
            pl.BlockSpec(memory_space=pltpu.HBM),
        ),
        scratch_shapes=[
            pltpu.VMEM((8, 64, 128), BF16),
            row,
            row,
            pltpu.VMEM((128, 256), BF16),
            pltpu.VMEM((128, 256), BF16),
            row,
            row,
            pltpu.VMEM((1024 + 16, 128), F32),
            pltpu.VMEM((512, 128), BF16),
            pltpu.VMEM((2, 128, 128), F32),
            pltpu.SemaphoreType.DMA((9,)),
        ],
        compiler_params=params(63),
        name="edges",
    )(
        pair,
        gain.reshape(1, 128),
        bias.reshape(1, 128),
        left_weight,
        right_weight,
        last_gain.reshape(1, 128),
        last_bias.reshape(1, 128),
    )


def pack_kernel(edges, pair, payload):
    left = edges[:, :8].reshape(512, 128)
    for target in range(4):
        payload[target, :512] = left
        payload[target, 512:] = pair[:, target * 16 : target * 16 + 16].reshape(128, 128)


def make_pack(edges, pair):
    return pl.pallas_call(
        pack_kernel,
        out_shape=jax.ShapeDtypeStruct((4, 640, 128), BF16),
        compiler_params=params(),
        name="pack",
    )(edges, pair)


def triangle_kernel(place, received, right, other, gate_weight, out, gates, normed, rows):
    first_core = place[0] % 2 == 0
    total = jnp.zeros((256, 256), F32)
    for part in range(8):
        mine = right[part * 64 : part * 64 + 64].astype(F32)
        theirs = other[part * 64 : part * 64 + 64].astype(F32)
        low = lane_mask(mine.shape)
        sides = (jnp.where(first_core, mine, theirs), jnp.where(first_core, theirs, mine))
        halves = [jnp.where(low, side, 0.0) for side in sides]
        halves += [jnp.where(low, 0.0, side) for side in sides]
        right_rows = jnp.concatenate(
            [half[a * 8 : a * 8 + 8] for a in range(8) for half in halves], axis=0
        ).astype(BF16)
        held = received[:, part * 64 : part * 64 + 64].astype(F32)
        left_rows = jnp.concatenate(
            [held[y, a * 8 : a * 8 + 8] for a in range(8) for y in range(4)], axis=0
        ).astype(BF16)
        total += lax.dot_general(
            right_rows, left_rows, (((1,), (1,)), ((), ())), preferred_element_type=F32
        )
    lane_group = lax.broadcasted_iota(jnp.int32, (64, 128), 1) // 32
    for block in range(2):
        rows[block, :256] = total[:, block * 128 : block * 128 + 128]
        taken = [rows[block, pl.ds(row, 64, stride=4), :] for row in range(4)]
        for group in range(4):
            turned = taken[0] if group == 0 else pltpu.roll(taken[0], 128 - group * 32, 1)
            for row in range(1, 4):
                shift = (row - group) * 32 % 128
                rolled = pltpu.roll(taken[row], shift, 1) if shift else taken[row]
                turned = jnp.where(lane_group == row, rolled, turned)
            turned = turned.astype(BF16).reshape(8, 8, 128)
            for target in range(8):
                out[PLACES[target][block * 4 + group], target] = turned[target]
    normed[:512] = received[:, 512:].astype(F32).reshape(512, 128)
    for part in range(4):
        first = part // 2 * 8 + part % 2 * 4
        pairs = jnp.concatenate(
            [normed[pl.ds(first + row, 32, stride=16), :] for row in range(4)], axis=0
        ).astype(BF16)
        logits = lax.dot_general(
            gate_weight[...], pairs, (((0,), (1,)), ((), ())), preferred_element_type=F32
        )
        gates[part] = jax.nn.sigmoid(logits)


def make_triangle(place, received, right, other, gate_weight):
    return pl.pallas_call(
        triangle_kernel,
        out_shape=(
            jax.ShapeDtypeStruct((8, 8, 8, 128), BF16),
            jax.ShapeDtypeStruct((4, 128, 128), F32),
        ),
        in_specs=[pl.BlockSpec(memory_space=pltpu.SMEM)]
        + [pl.BlockSpec(memory_space=pltpu.VMEM)] * 4,
        scratch_shapes=[pltpu.VMEM((512 + 16, 128), F32), pltpu.VMEM((2, 256 + 8, 128), F32)],
        compiler_params=params(),
        name="triangle",
    )(place, received, right, other, gate_weight)


def update_kernel(triangle, gates, out_weight, tall, out, scratch):
    values = triangle[...].astype(F32)
    sums = jnp.sum(values, axis=0)
    squares = jnp.sum(values * values, axis=0)
    center = (sums + pltpu.roll(sums, 4, 0)) / 128
    spread = (squares + pltpu.roll(squares, 4, 0)) / 128 - center * center
    scale = lax.rsqrt(spread + 1e-05)
    scratch[:512] = ((values - center) * scale).reshape(512, 128)
    for part in range(4):
        held = jnp.concatenate(
            [
                scratch[pl.ds(part, 64, stride=8), :],
                scratch[pl.ds(4 + part, 64, stride=8), :],
            ],
            axis=0,
        )
        held = (held * tall[0] + tall[1]).astype(BF16)
        projected = lax.dot_general(
            out_weight[...], held, (((0,), (0,)), ((), ())), preferred_element_type=F32
        )
        update = (gates[part] * projected).astype(BF16)
        out[:, part // 2, part % 2] = update.reshape(8, 16, 128)


def make_update(triangle, gates, out_weight, tall):
    return pl.pallas_call(
        update_kernel,
        out_shape=jax.ShapeDtypeStruct((8, 2, 2, 16, 128), BF16),
        scratch_shapes=[pltpu.VMEM((512 + 8, 128), F32)],
        compiler_params=params(),
        name="update",
    )(triangle, gates, out_weight, tall)


def order_matrix():
    lanes = np.arange(512).reshape(2, 2, 4, 4, 8).transpose(2, 0, 3, 1, 4).reshape(512)
    return (np.arange(512)[:, None] == lanes[None, :]).astype(jnp.bfloat16)


def order_kernel(place, update, matrix, out):
    own = place[0] // 8
    held = [PLACES[0][source] for source in range(8)]
    for target in range(1, 8):
        held = [
            jnp.where(own == target, PLACES[target][source], held[source]) for source in range(8)
        ]
    pieces = [
        jnp.concatenate(
            [update[held[block * 2 + side] * 2 + core, half] for side in range(2) for core in range(2)],
            axis=1,
        )
        for block in range(4)
        for half in range(2)
    ]
    turned = jnp.dot(
        jnp.concatenate(pieces, axis=0), matrix[...], preferred_element_type=F32
    ).astype(BF16)
    for block in range(4):
        for half in range(2):
            rows = (block * 2 + half) * 16
            for row in range(4):
                out[half * 4 + row, :, block * 128 : block * 128 + 128] = turned[
                    rows : rows + 16, row * 128 : row * 128 + 128
                ]


def make_order(place, update):
    return pl.pallas_call(
        order_kernel,
        out_shape=jax.ShapeDtypeStruct((8, 16, 512), BF16),
        in_specs=[
            pl.BlockSpec(memory_space=pltpu.SMEM),
            pl.BlockSpec(memory_space=pltpu.VMEM),
            pl.BlockSpec(memory_space=pltpu.VMEM),
        ],
        compiler_params=params(),
        name="order",
    )(place, update, jnp.asarray(order_matrix()))


def exchange(values, axes):
    return lax.all_to_all(values, axes, 0, 0, tiled=True)


def shards(
    pair_rep,
    pair_gain,
    pair_bias,
    left_weight,
    right_weight,
    gate_weight,
    out_weight,
    out_gain,
    out_bias,
):
    swapped = [
        ((s * 8 + e) * 8 + t, (t * 8 + e) * 8 + PLACES[t][s])
        for s in range(8)
        for e in range(8)
        for t in range(8)
    ]
    place = lax.axis_index(AXES[:4]).astype(jnp.int32).reshape(1)
    edges, normed, tall = make_edges(
        pair_rep, pair_gain, pair_bias, left_weight, right_weight, out_gain, out_bias
    )
    moved = lax.ppermute(normed.reshape(8, 64, 128), AXES, swapped)
    edges = lax.cond(
        lax.axis_index("x") < 4,
        lambda held: exchange(held, SPLIT),
        lambda held: held,
        edges.reshape(64, 16, 128),
    )
    received = exchange(make_pack(edges, moved), "y")
    right = edges[:, 8:].reshape(512, 128)
    other = lax.ppermute(right, "co", [(0, 1), (1, 0)])
    triangle, gates = make_triangle(place, received, right, other, gate_weight)
    triangle = exchange(triangle.reshape(64, 8, 128), SPLIT)
    update = make_update(triangle, gates, out_weight, tall)
    return make_order(place, exchange(update.reshape(16, 2, 16, 128), ("n", "co")))


def solution(mesh):
    fine = Mesh(mesh.devices.reshape(4, 2, 4, 2, 8), AXES)
    rows = ("x", "zh", "y", "co")
    in_specs = (P(rows, "n", None), P(), P(), P(), P(), P(), P(), P(), P())
    out_specs = P(rows, "n", None)
    return jax.shard_map(shards, mesh=fine, in_specs=in_specs, out_specs=out_specs, check_vma=False)
```
